512 devices in a mesh: ctx: 64 (over y_hi, z, core), tp: 8 (over y_lo, x).
Axes of the slice: x: 4, y: 4 (y_hi: 2, y_lo: 2; y = y_hi * 2 + y_lo), z: 16, core: 2. Of those that a mesh axis runs over, the one named last changes fastest.
Arguments:
- context_query: bfloat16 [65536, 32, 128], P('ctx', 'tp'), may hold values from -140 to 140
- context_pairs: bfloat16 [65536, 8, 2, 128], P('ctx', 'tp'), may hold values from -6 to 6
- anchor_block: int32 [1], replicated, may hold values from 0 to 63
- answer_query: bfloat16 [64, 32, 128], P('ctx', 'tp'), may hold values from -256 to 256
- answer_pairs: bfloat16 [64, 8, 2, 128], P('ctx', 'tp'), may hold values from -6 to 6
- output_weight: bfloat16 [4096, 8192], P('tp', 'ctx'), may hold values from -0.09375 to 0.09375
Outputs:
- context_heads: bfloat16 [65536, 32, 128], P('ctx', 'tp')
- answer_output: bfloat16 [64, 8192], P('tp', 'ctx')
The draws below stay inside these ranges and needn't reach their ends.
All inputs are finite; a program needn't handle non-finite values.
Results may differ from the reference program's by a relative error of at most 0.019.
Values may be sent and summed in bfloat16 or wider, within the bound.
A program may use at most 64 MiB of HBM per device.

```python
import jax
import jax.numpy as jnp
from jax import lax

HD = 128
GROUP = 4
KV_HEADS = 8
HQ = 32
BLOCK = 1024
QTOK = 64
D = 8192
TOKENS = 65536
N_CTX = 64


def shared_pairs(key):
    return jnp.clip(jax.random.normal(key, (TOKENS, KV_HEADS, 2, HD), jnp.float32), -6.0, 6.0)


def draw_context_pairs(key, part):
    return shared_pairs(key).astype(jnp.bfloat16)


def draw_context_query(key, part):
    key = jax.random.fold_in(key, 7)
    values = jnp.clip(2.5 * jax.random.normal(key, (TOKENS, HQ, HD), jnp.float32), -15.0, 15.0)
    return values.astype(jnp.bfloat16)


def draw_answer_query(key, part):
    key = jax.random.fold_in(key, 13)
    values = jnp.clip(2.5 * jax.random.normal(key, (QTOK, HQ, HD), jnp.float32), -15.0, 15.0)
    return values.astype(jnp.bfloat16)


def levels(stream_key, extent, cuts, smallest, largest):
    def one(axis_at, parts):
        steps = jax.random.uniform(jax.random.fold_in(jax.random.fold_in(stream_key, 6), axis_at), (parts,), jnp.float32, smallest / len(cuts), largest / len(cuts))
        return jnp.repeat(jnp.exp(steps), extent[axis_at] // parts).reshape((-1,) + (1,) * (len(extent) - axis_at - 1))

    gain = one(*cuts[0])
    for cut in cuts[1:]:
        gain = gain * one(*cut)
    return gain


def centred(key, extent, deviation, most, cuts=(), kind=jnp.bfloat16):
    array = jax.random.normal(key, extent, jnp.float32) * deviation
    if len(cuts) > 0:
        array = levels(key, extent, cuts, -0.22, 0.18) * array
    return jnp.clip(array, min=-most, max=most).astype(kind)


def setup_inputs(seed: int = 0) -> dict:
    seeds = jax.random.split(jax.random.key(seed), 7)
    context_query = draw_context_query(jax.random.fold_in(seeds[6], 71), 0)
    context_pairs = draw_context_pairs(jax.random.fold_in(seeds[6], 71), 0)
    anchor_block = jax.random.randint(seeds[2], (1,), 0, N_CTX).astype(jnp.int32)
    answer_query = draw_answer_query(jax.random.fold_in(seeds[6], 71), 0)
    answer_pairs = centred(seeds[4], (QTOK, KV_HEADS, 2, HD), 1.0, 6.0, ((0, 64), (1, 8)))
    output_weight = centred(seeds[5], (HQ * HD, D), (HQ * HD) ** -0.5, 0.09375, ((0, 8), (1, 64)))
    return dict(context_query=context_query, context_pairs=context_pairs, anchor_block=anchor_block, answer_query=answer_query, answer_pairs=answer_pairs, output_weight=output_weight)


def block_attention(block_query, own_pairs, anchor_pairs, is_anchor):
    query = block_query.astype(jnp.float32)
    own_keys = own_pairs[:, :, 0, :].astype(jnp.float32)
    own_values = own_pairs[:, :, 1, :].astype(jnp.float32)
    far_keys = anchor_pairs[:, :, 0, :].astype(jnp.float32)
    far_values = anchor_pairs[:, :, 1, :].astype(jnp.float32)
    score_scale = HD ** -0.5
    own_scores = jnp.einsum('tghd,sgd->ghts', query, own_keys) * score_scale
    far_scores = jnp.einsum('tghd,sgd->ghts', query, far_keys) * score_scale
    positions = jnp.arange(BLOCK)
    causal = positions[None, :] <= positions[:, None]
    own_scores = jnp.where(causal, own_scores, -jnp.inf)
    far_scores = jnp.where(is_anchor, -jnp.inf, far_scores)
    peak = jnp.maximum(jnp.max(own_scores, axis=-1), jnp.max(far_scores, axis=-1))
    own_probs = jnp.exp(own_scores - peak[..., None])
    far_probs = jnp.exp(far_scores - peak[..., None])
    weight_sum = jnp.sum(own_probs, axis=-1) + jnp.sum(far_probs, axis=-1)
    mixed = jnp.einsum('ghts,sgd->tghd', own_probs.astype(jnp.bfloat16).astype(jnp.float32), own_values)
    mixed = mixed + jnp.einsum('ghts,sgd->tghd', far_probs.astype(jnp.bfloat16).astype(jnp.float32), far_values)
    mixed = mixed / jnp.transpose(weight_sum, (2, 0, 1))[..., None]
    return mixed.astype(jnp.bfloat16)


def answer_group(inputs):
    group_query, context_group, self_group = inputs
    query = group_query.astype(jnp.float32)
    score_scale = HD ** -0.5
    far_scores = jnp.einsum('qhd,sd->hqs', query, context_group[0].astype(jnp.float32)) * score_scale
    self_scores = jnp.einsum('qhd,sd->hqs', query, self_group[0].astype(jnp.float32)) * score_scale
    positions = jnp.arange(QTOK)
    causal = positions[None, :] <= positions[:, None]
    self_scores = jnp.where(causal[None], self_scores, -jnp.inf)
    peak = jnp.maximum(jnp.max(far_scores, axis=-1), jnp.max(self_scores, axis=-1))
    far_probs = jnp.exp(far_scores - peak[..., None])
    self_probs = jnp.exp(self_scores - peak[..., None])
    weight_sum = jnp.sum(far_probs, axis=-1) + jnp.sum(self_probs, axis=-1)
    mixed = jnp.einsum('hqs,sd->hqd', far_probs.astype(jnp.bfloat16).astype(jnp.float32), context_group[1].astype(jnp.float32))
    mixed = mixed + jnp.einsum('hqs,sd->hqd', self_probs.astype(jnp.bfloat16).astype(jnp.float32), self_group[1].astype(jnp.float32))
    mixed = mixed / weight_sum[..., None]
    return jnp.transpose(mixed, (1, 0, 2)).astype(jnp.bfloat16)


def reference(context_query, context_pairs, anchor_block, answer_query, answer_pairs, output_weight):
    kv_count = context_pairs.shape[1]
    blocks_query = context_query.reshape(N_CTX, BLOCK, kv_count, GROUP, HD)
    blocks_pairs = context_pairs.reshape(N_CTX, BLOCK, kv_count, 2, HD)
    anchor_index = anchor_block[0].astype(jnp.int32)
    anchor_pairs = lax.dynamic_index_in_dim(blocks_pairs, anchor_index, 0, keepdims=False)

    def one_block(inputs):
        block_query, own_pairs, block_index = inputs
        return block_attention(block_query, own_pairs, anchor_pairs, block_index == anchor_index)

    block_outputs = lax.map(one_block, (blocks_query, blocks_pairs, jnp.arange(N_CTX, dtype=jnp.int32)))
    context_heads = block_outputs.reshape(TOKENS, kv_count * GROUP, HD)

    grouped_query = jnp.transpose(answer_query.reshape(QTOK, kv_count, GROUP, HD), (1, 0, 2, 3))
    context_groups = jnp.transpose(context_pairs, (1, 2, 0, 3))
    self_groups = jnp.transpose(answer_pairs, (1, 2, 0, 3))
    answer_heads = lax.map(answer_group, (grouped_query, context_groups, self_groups))
    answer_flat = jnp.transpose(answer_heads, (1, 0, 2, 3)).reshape(QTOK, kv_count * GROUP * HD)
    answer_output = jnp.dot(answer_flat, output_weight, preferred_element_type=jnp.float32).astype(jnp.bfloat16)
    return context_heads, answer_output
```

```python
import functools
import math

import jax
import jax.numpy as jnp
from jax import lax
from jax.experimental import pallas as pl
from jax.experimental.pallas import tpu as pltpu
from jax.sharding import PartitionSpec as P

MESH = pl.DeviceIdType.MESH
N_CTX, N_TP, N_Z = 64, 8, 16
HD, GROUP, BLOCK, QTOK = 128, 4, 1024, 64
ROWS = BLOCK * GROUP
SUB = 256
F32, BF16 = jnp.float32, jnp.bfloat16
C2 = HD**-0.5 * math.log2(math.e)


def dot_t(a, b):
    return lax.dot_general(a, b, (((1,), (1,)), ((), ())), preferred_element_type=F32)


def kernel(
    anchor_ref, q_hbm, pairs_hbm, aq_hbm, ap_hbm, w_hbm,
    out_hbm, ans_ref,
    q_v, pairs_v, pairs_f, aq_ref, ap_ref, w_v, out_v,
    kv_own, k_cand, v_cand, z_src, kz_cand, vz_cand, far,
    m_s, l_s, acc_s,
    q_all, akv, o_f, o_src, l_src, o_recv, l_recv, h_src, h_all, p_src, p_recv,
    load_sem, store_sem, send_sem, recv_sem,
):
    c = lax.axis_index("ctx")
    p = lax.axis_index("tp")
    y, z, k = c // 32, (c // 2) % N_Z, c % 2
    rank = 2 * y + k

    def ctx_at(y, z, k):
        return (y * N_Z + z) * 2 + k

    anchor = anchor_ref[0]
    a_rank, a_z = 2 * (anchor // 32) + anchor % 2, (anchor // 2) % N_Z
    is_anchor = anchor == c

    loads = [
        pltpu.make_async_copy(pairs_hbm, pairs_v, load_sem.at[0]),
        pltpu.make_async_copy(q_hbm, q_v, load_sem.at[1]),
        pltpu.make_async_copy(w_hbm, w_v, load_sem.at[2]),
        pltpu.make_async_copy(aq_hbm, aq_ref, load_sem.at[3]),
        pltpu.make_async_copy(ap_hbm, ap_ref, load_sem.at[4]),
    ]
    for load in loads:
        load.start()
    barrier = pltpu.get_barrier_semaphore()
    for d in range(1, N_CTX):
        pl.semaphore_signal(barrier, inc=1, device_id={"ctx": (c + d) % N_CTX}, device_id_type=MESH)
    for d in range(1, N_TP):
        pl.semaphore_signal(barrier, inc=1, device_id={"tp": (p + d) % N_TP}, device_id_type=MESH)

    loads[0].wait()
    pairs_f[...] = pairs_v[...].astype(F32)
    for kv in range(2):
        kv_own[kv] = pairs_f[pl.ds(kv, BLOCK, stride=2), :].astype(BF16).reshape(4, N_Z, 16, HD)
    loads[3].wait()
    loads[4].wait()
    q_all[c] = aq_ref[0]
    pl.semaphore_wait(barrier, N_CTX - 1 + N_TP - 1)

    def send(src, dst, sem, **device):
        pltpu.make_async_remote_copy(
            src_ref=src, dst_ref=dst, send_sem=send_sem.at[sem], recv_sem=recv_sem.at[sem],
            device_id=device, device_id_type=MESH,
        ).start()

    def arrived(ref, sem):
        pltpu.make_async_copy(ref, ref, recv_sem.at[sem]).wait()

    def sent(ref, sem):
        pltpu.make_async_copy(ref, ref, send_sem.at[sem]).wait()

    near = [(y, 1 - k), (1 - y, k), (1 - y, 1 - k)]
    near_cand, z_cand = (k_cand, v_cand), (kz_cand, vz_cand)

    def near_scatter(kv):
        for to_y, to_k in near:
            to = 2 * to_y + to_k
            send(kv_own.at[kv, to], near_cand[kv].at[rank], kv, ctx=ctx_at(to_y, z, to_k))
        near_cand[kv][rank] = kv_own[kv, rank]

    def z_scatter(kv):
        arrived(near_cand[kv].at[pl.ds(0, 3)], kv)
        z_src[kv] = near_cand[kv][a_rank]
        for d in range(1, N_Z):
            to = (z + d) % N_Z
            send(z_src.at[kv, to], z_cand[kv].at[z], 2 + kv, ctx=ctx_at(y, to, k))
        z_cand[kv][z] = z_src[kv, z]

    def z_gather(kv):
        arrived(z_cand[kv].at[pl.ds(0, N_Z - 1)], 2 + kv)
        far[kv, rank, z] = z_cand[kv][a_z]
        for d in range(1, N_Z):
            to = (z + d) % N_Z
            send(far.at[kv, rank, z], far.at[kv, rank, z], 4 + kv, ctx=ctx_at(y, to, k))

    def near_gather(kv):
        arrived(far.at[kv, 0, pl.ds(0, N_Z - 1)], 4 + kv)
        for to_y, to_k in near:
            send(far.at[kv, rank], far.at[kv, rank], 6 + kv, ctx=ctx_at(to_y, z, to_k))

    def far_here(kv):
        arrived(far.at[kv, pl.ds(0, 3)], 6 + kv)

    def own_part(i):
        keys = kv_own[0, 0 : i + 1].reshape((i + 1) * 256, HD)
        values = kv_own[1, 0 : i + 1].reshape((i + 1) * 256, HD)

        def step(j, _):
            rows = pl.ds(pl.multiple_of(i * 1024 + j * SUB, SUB), SUB)
            scores = dot_t(q_v[rows, :], keys)
            token = lax.broadcasted_iota(jnp.int32, (SUB, 256), 0) // GROUP + j * (SUB // GROUP)
            seen = lax.broadcasted_iota(jnp.int32, (SUB, 256), 1) <= token
            last = jnp.where(seen, scores[:, i * 256 :], -jnp.inf)
            scores = jnp.concatenate([scores[:, : i * 256], last], axis=1) if i else last
            peak = jnp.max(scores, axis=1, keepdims=True)
            probs = jnp.exp2((scores - peak) * C2)
            m_s[rows, :] = peak
            l_s[rows, :] = jnp.sum(probs, axis=1, keepdims=True)
            acc_s[rows, :] = jnp.dot(probs.astype(BF16), values, preferred_element_type=F32)
            return 0

        lax.fori_loop(0, 1024 // SUB, step, 0)

    def far_part():
        keys = far[0].reshape(BLOCK, HD)
        values = far[1].reshape(BLOCK, HD)
        far_weight = jnp.where(is_anchor, 0.0, 1.0).astype(F32)

        def step(j, _):
            rows = pl.ds(pl.multiple_of(j * SUB, SUB), SUB)
            scores = dot_t(q_v[rows, :], keys)
            own_peak = m_s[rows, :]
            peak = jnp.maximum(own_peak, jnp.max(scores, axis=1, keepdims=True))
            probs = jnp.exp2((scores - peak) * C2)
            rescale = jnp.where(is_anchor, 1.0, jnp.exp2((own_peak - peak) * C2))
            weight_sum = l_s[rows, :] * rescale + far_weight * jnp.sum(probs, axis=1, keepdims=True)
            mixed = acc_s[rows, :] * rescale + far_weight * jnp.dot(
                probs.astype(BF16), values, preferred_element_type=F32
            )
            out_v[rows, :] = (mixed / weight_sum).astype(BF16)
            return 0

        lax.fori_loop(0, ROWS // SUB, step, 0)

    def answer_part():
        arrived(q_all.at[pl.ds(0, N_CTX - 1)], 8)
        o_f[...] = q_all[...].astype(F32)
        queries = jnp.concatenate([o_f[:, h, :] for h in range(GROUP)], axis=0).astype(BF16)
        scores = dot_t(queries, kv_own[0].reshape(BLOCK, HD))
        peak = jnp.max(scores, axis=1, keepdims=True)
        probs = jnp.exp2((scores - peak) * C2)
        weight_sum = jnp.sum(probs, axis=1, keepdims=True)
        mixed = jnp.dot(
            probs.astype(BF16), kv_own[1].reshape(BLOCK, HD), preferred_element_type=F32
        )
        return queries, peak, weight_sum, mixed

    def answer_self(queries, peak, weight_sum, mixed):
        arrived(akv.at[pl.ds(0, N_CTX - 1)], 9)
        pairs = akv[...].astype(F32)
        scores = dot_t(queries, pairs[:, 0, :].astype(BF16))
        token = lax.broadcasted_iota(jnp.int32, (GROUP * QTOK, QTOK), 0) % QTOK
        seen = lax.broadcasted_iota(jnp.int32, (GROUP * QTOK, QTOK), 1) <= token
        scores = jnp.where(seen, scores, -jnp.inf)
        both = jnp.maximum(peak, jnp.max(scores, axis=1, keepdims=True))
        rescale = jnp.exp2((peak - both) * C2)
        probs = jnp.exp2((scores - both) * C2)
        weight_sum = weight_sum * rescale + jnp.sum(probs, axis=1, keepdims=True)
        mixed = mixed * rescale + jnp.dot(
            probs.astype(BF16), pairs[:, 1, :].astype(BF16), preferred_element_type=F32
        )
        return both, weight_sum, mixed

    def answer_scatter():
        queries, peak, weight_sum, mixed = answer_part()
        peak, weight_sum, mixed = lax.cond(
            c == 0,
            lambda: answer_self(queries, peak, weight_sum, mixed),
            lambda: (peak, weight_sum, mixed),
        )
        level = peak * C2 + jnp.log2(weight_sum)
        mixed = mixed / weight_sum
        lane = lax.broadcasted_iota(jnp.int32, (QTOK, HD), 1) // 32
        levels = jnp.zeros((QTOK, HD), F32)
        for h in range(GROUP):
            o_f[:, h, :] = mixed[h * QTOK : (h + 1) * QTOK]
            levels = jnp.where(lane == h, level[h * QTOK : (h + 1) * QTOK], levels)
        o_src[...] = o_f[...].astype(BF16)
        l_src[...] = levels.reshape(QTOK, 1, HD)
        for d in range(1, N_CTX):
            to = (c + d) % N_CTX
            send(o_src.at[to], o_recv.at[c], 10, ctx=to)
            send(l_src.at[to], l_recv.at[c], 11, ctx=to)
        o_recv[c] = o_src[c]
        l_recv[c] = l_src[c]

    def answer_merge():
        arrived(o_recv.at[pl.ds(0, N_CTX - 1)], 10)
        arrived(l_recv.at[pl.ds(0, N_CTX - 1)], 11)
        o_f[...] = o_recv[...].astype(F32)
        level = l_recv[...].reshape(N_CTX, HD)
        weight = jnp.exp2(level - jnp.max(level, axis=0, keepdims=True))
        heads = []
        for h in range(GROUP):
            part = weight[:, 32 * h : 32 * h + 1]
            mixed = jnp.sum(o_f[:, h, :] * part, axis=0, keepdims=True)
            heads.append(mixed / jnp.sum(part, axis=0, keepdims=True))
        h_src[...] = jnp.concatenate(heads, axis=0).astype(BF16)
        for d in range(1, N_CTX):
            send(h_src, h_all.at[c], 12, ctx=(c + d) % N_CTX)
        h_all[c] = h_src[...]

    def answer_project():
        arrived(h_all.at[pl.ds(0, N_CTX - 1)], 12)
        o_f[...] = h_all[...].astype(F32)
        flat = jnp.concatenate([o_f[:, h, :] for h in range(GROUP)], axis=1).astype(BF16)
        share = jnp.dot(flat, w_v[...], preferred_element_type=F32)
        p_src[...] = share.reshape(N_TP, QTOK // N_TP, HD)
        for d in range(1, N_TP):
            to = (p + d) % N_TP
            send(p_src.at[to], p_recv.at[p], 13, tp=to)
        p_recv[p] = p_src[p]
        arrived(p_recv.at[pl.ds(0, N_TP - 1)], 13)
        ans_ref[...] = jnp.sum(p_recv[...], axis=0).astype(BF16)

    for d in range(1, N_CTX):
        send(aq_ref.at[0], q_all.at[c], 8, ctx=(c + d) % N_CTX)
    near_scatter(0)
    near_scatter(1)

    @pl.when(c != 0)
    def _():
        send(ap_ref.at[0], akv.at[c], 9, ctx=0)

    @pl.when(c == 0)
    def _():
        akv[0] = ap_ref[0]

    loads[1].wait()
    own_part(0)
    own_part(1)
    own_part(2)
    z_scatter(0)
    z_scatter(1)
    own_part(3)
    answer_scatter()
    z_gather(0)
    z_gather(1)
    near_gather(0)
    answer_merge()
    near_gather(1)
    far_here(0)
    far_here(1)
    far_part()
    store = pltpu.make_async_copy(out_v, out_hbm, store_sem)
    store.start()
    loads[2].wait()
    answer_project()

    for kv in range(2):
        sent(near_cand[kv].at[pl.ds(0, 3)], kv)
        sent(z_cand[kv].at[pl.ds(0, N_Z - 1)], 2 + kv)
        sent(far.at[kv, 0, pl.ds(0, N_Z - 1)], 4 + kv)
        sent(far.at[kv, pl.ds(0, 3)], 6 + kv)
    sent(q_all.at[pl.ds(0, N_CTX - 1)], 8)

    @pl.when(c != 0)
    def _():
        sent(akv.at[0], 9)

    sent(o_recv.at[pl.ds(0, N_CTX - 1)], 10)
    sent(l_recv.at[pl.ds(0, N_CTX - 1)], 11)
    sent(h_all.at[pl.ds(0, N_CTX - 1)], 12)
    sent(p_recv.at[pl.ds(0, N_TP - 1)], 13)
    store.wait()


def on_device(
    context_query, context_pairs, anchor_block, answer_query, answer_pairs, output_weight
):
    hbm = pl.BlockSpec(memory_space=pltpu.HBM)
    any_space = pl.BlockSpec(memory_space=pl.ANY)
    vmem = pl.BlockSpec(memory_space=pltpu.VMEM)
    out, answer_output = pl.pallas_call(
        kernel,
        out_shape=(
            jax.ShapeDtypeStruct((ROWS, HD), BF16),
            jax.ShapeDtypeStruct((QTOK // N_TP, HD), BF16),
        ),
        in_specs=[pl.BlockSpec(memory_space=pltpu.SMEM), hbm, hbm, hbm, hbm, hbm],
        out_specs=(any_space, vmem),
        scratch_shapes=[
            pltpu.VMEM((ROWS, HD), BF16),
            pltpu.VMEM((2 * BLOCK, HD), BF16),
            pltpu.VMEM((2 * BLOCK, HD), F32),
            pltpu.VMEM((1, GROUP, HD), BF16),
            pltpu.VMEM((1, 2, HD), BF16),
            pltpu.VMEM((GROUP * HD, HD), BF16),
            pltpu.VMEM((ROWS, HD), BF16),
            pltpu.VMEM((2, 4, N_Z, 16, HD), BF16),
            pltpu.VMEM((4, N_Z, 16, HD), BF16),
            pltpu.VMEM((4, N_Z, 16, HD), BF16),
            pltpu.VMEM((2, N_Z, 16, HD), BF16),
            pltpu.VMEM((N_Z, 16, HD), BF16),
            pltpu.VMEM((N_Z, 16, HD), BF16),
            pltpu.VMEM((2, 4, N_Z, 16, HD), BF16),
            pltpu.VMEM((ROWS, 1), F32),
            pltpu.VMEM((ROWS, 1), F32),
            pltpu.VMEM((ROWS, HD), F32),
            pltpu.VMEM((N_CTX, GROUP, HD), BF16),
            pltpu.VMEM((N_CTX, 2, HD), BF16),
            pltpu.VMEM((N_CTX, GROUP, HD), F32),
            pltpu.VMEM((N_CTX, GROUP, HD), BF16),
            pltpu.VMEM((N_CTX, 1, HD), F32),
            pltpu.VMEM((N_CTX, GROUP, HD), BF16),
            pltpu.VMEM((N_CTX, 1, HD), F32),
            pltpu.VMEM((GROUP, HD), BF16),
            pltpu.VMEM((N_CTX, GROUP, HD), BF16),
            pltpu.VMEM((N_TP, QTOK // N_TP, HD), F32),
            pltpu.VMEM((N_TP, QTOK // N_TP, HD), F32),
            pltpu.SemaphoreType.DMA((5,)),
            pltpu.SemaphoreType.DMA,
            pltpu.SemaphoreType.DMA((14,)),
            pltpu.SemaphoreType.DMA((14,)),
        ],
        compiler_params=pltpu.CompilerParams(
            collective_id=0, has_side_effects=True, vmem_limit_bytes=60 * 1024 * 1024
        ),
        cost_estimate=pl.CostEstimate(
            flops=4 * ROWS * BLOCK * HD * 2, bytes_accessed=1 << 22, transcendentals=2 * ROWS * BLOCK
        ),
        name="two_phase_attention",
    )(
        anchor_block,
        context_query.reshape(ROWS, HD),
        context_pairs.reshape(2 * BLOCK, HD),
        answer_query,
        answer_pairs.reshape(1, 2, HD),
        output_weight,
    )
    return out.reshape(BLOCK, GROUP, HD), answer_output


def solution(mesh):
    in_specs = (
        P("ctx", "tp", None),
        P("ctx", "tp", None, None),
        P(),
        P("ctx", "tp", None),
        P("ctx", "tp", None, None),
        P("tp", "ctx"),
    )
    out_specs = (P("ctx", "tp", None), P("tp", "ctx"))
    return jax.shard_map(
        on_device, mesh=mesh, in_specs=in_specs, out_specs=out_specs, check_vma=False
    )
```

```python
import functools
import math

import jax
import jax.numpy as jnp
from jax import lax
from jax.experimental import pallas as pl
from jax.experimental.pallas import tpu as pltpu
from jax.sharding import PartitionSpec as P

MESH = pl.DeviceIdType.MESH
N_CTX, N_TP, N_Z = 64, 8, 16
HD, GROUP, BLOCK, QTOK = 128, 4, 1024, 64
ROWS = BLOCK * GROUP
COLS = 1024
F32, BF16 = jnp.float32, jnp.bfloat16
C2 = HD**-0.5 * math.log2(math.e)


def dot_t(a, b):
    return lax.dot_general(a, b, (((1,), (1,)), ((), ())), preferred_element_type=F32)


def kernel(
    anchor_ref, q_hbm, pairs_hbm, aq_hbm, ap_hbm, w_hbm,
    out_ref, ans_ref,
    q_v, pairs_v, pairs_f, w_v, own_k, own_vt,
    cand_0, cand_1, z_src, z_cand_0, z_cand_1, far_0, far_1, far_f, far_k, far_vt,
    m_s, l_s, acc_s,
    q_all, akv, o_src, l_src, o_recv, l_recv,
    o2_src, l2_src, o2_recv, l2_recv, h_src, h_all, h_f, p_src, p_recv,
    load_sem, send_sem, recv_sem,
):
    c = lax.axis_index("ctx")
    p = lax.axis_index("tp")
    y, z, k = c // 32, (c // 2) % N_Z, c % 2
    rank = 2 * y + k
    z_hi, z_lo = z // 4, z % 4
    local = 4 * z_lo + rank

    def ctx_at(y, z, k):
        return (y * N_Z + z) * 2 + k

    anchor = anchor_ref[0]
    a_rank, a_z = 2 * (anchor // 32) + anchor % 2, (anchor // 2) % N_Z
    is_anchor = anchor == c

    barrier = pltpu.get_barrier_semaphore()
    for d in range(1, N_CTX):
        pl.semaphore_signal(barrier, inc=1, device_id={"ctx": (c + d) % N_CTX}, device_id_type=MESH)
    for d in range(1, N_TP):
        pl.semaphore_signal(barrier, inc=1, device_id={"tp": (p + d) % N_TP}, device_id_type=MESH)
    loads = [
        pltpu.make_async_copy(pairs_hbm, pairs_v, load_sem.at[0]),
        pltpu.make_async_copy(q_hbm, q_v, load_sem.at[1]),
        pltpu.make_async_copy(w_hbm, w_v, load_sem.at[2]),
        pltpu.make_async_copy(aq_hbm.at[0], q_all.at[c], load_sem.at[3]),
    ]
    for load in loads:
        load.start()
    pl.semaphore_wait(barrier, N_CTX - 1 + N_TP - 1)

    def send(src, dst, sem, **device):
        pltpu.make_async_remote_copy(
            src_ref=src, dst_ref=dst, send_sem=send_sem.at[sem], recv_sem=recv_sem.at[sem],
            device_id=device, device_id_type=MESH,
        ).start()

    def arrived(ref, sem):
        pltpu.make_async_copy(ref, ref, recv_sem.at[sem]).wait()

    def sent(ref, sem):
        pltpu.make_async_copy(ref, ref, send_sem.at[sem]).wait()

    near = [(y, 1 - k), (1 - y, k), (1 - y, 1 - k)]
    cand, z_cand, far = (cand_0, cand_1), (z_cand_0, z_cand_1), (far_0, far_1)

    def near_scatter(half):
        for to_y, to_k in near:
            to = 2 * to_y + to_k
            send(pairs_hbm.at[to, half], cand[half].at[rank], half, ctx=ctx_at(to_y, z, to_k))

    def z_scatter(half):
        cand[half][rank] = pairs_v[rank, half]
        arrived(cand[half].at[pl.ds(0, 3)], half)
        z_src[half] = cand[half][a_rank]
        for d in range(1, N_Z):
            to = (z + d) % N_Z
            send(z_src.at[half, to], z_cand[half].at[z], 2 + half, ctx=ctx_at(y, to, k))
        z_cand[half][z] = z_src[half, z]

    def z_gather(half):
        arrived(z_cand[half].at[pl.ds(0, N_Z - 1)], 2 + half)
        far[half][rank, z] = z_cand[half][a_z]
        for d in range(1, N_Z):
            to = (z + d) % N_Z
            send(far[half].at[rank, z], far[half].at[rank, z], 4 + half, ctx=ctx_at(y, to, k))

    def near_gather(half):
        arrived(far[half].at[0, pl.ds(0, N_Z - 1)], 4 + half)
        for to_y, to_k in near:
            send(far[half].at[rank], far[half].at[rank], 6 + half, ctx=ctx_at(to_y, z, to_k))

    def own_part(i):
        cols = slice(i * COLS, (i + 1) * COLS)
        scores = dot_t(own_k[0 : (i + 1) * 256, :], q_v[cols, :])
        token = lax.broadcasted_iota(jnp.int32, (256, COLS), 1) // GROUP
        seen = lax.broadcasted_iota(jnp.int32, (256, COLS), 0) <= token
        last = jnp.where(seen, scores[i * 256 :], -jnp.inf)
        scores = jnp.concatenate([scores[: i * 256], last], axis=0) if i else last
        peak = jnp.max(scores, axis=0, keepdims=True)
        probs = jnp.exp2((scores - peak) * C2)
        m_s[:, cols] = peak
        l_s[:, cols] = jnp.sum(probs, axis=0, keepdims=True)
        acc_s[:, cols] = jnp.dot(
            own_vt[:, 0 : (i + 1) * 256], probs.astype(BF16), preferred_element_type=F32
        )

    def far_here(half):
        arrived(far[half].at[pl.ds(0, 3)], 6 + half)
        far_f[...] = far[half][...].reshape(BLOCK, HD).astype(F32)
        far_k[...] = far_f[pl.ds(0, BLOCK // 2, stride=2), :].astype(BF16)
        far_vt[...] = far_f[pl.ds(1, BLOCK // 2, stride=2), :].astype(BF16).T

    def far_part(blocks, last):
        far_weight = jnp.where(is_anchor, 0.0, 1.0).astype(F32)
        for i in blocks:
            cols = slice(i * COLS, (i + 1) * COLS)
            scores = dot_t(far_k[...], q_v[cols, :])
            before = m_s[:, cols]
            peak = jnp.maximum(before, jnp.max(scores, axis=0, keepdims=True))
            probs = jnp.exp2((scores - peak) * C2)
            rescale = jnp.where(is_anchor, 1.0, jnp.exp2((before - peak) * C2))
            weight_sum = l_s[:, cols] * rescale + far_weight * jnp.sum(probs, axis=0, keepdims=True)
            mixed = acc_s[:, cols] * rescale + far_weight * jnp.dot(
                far_vt[...], probs.astype(BF16), preferred_element_type=F32
            )
            if last:
                out_ref[cols, :] = (mixed / weight_sum).T.astype(BF16)
            else:
                m_s[:, cols] = peak
                l_s[:, cols] = weight_sum
                acc_s[:, cols] = mixed


    def answer_self(queries, peak, weight_sum, mixed):
        arrived(akv.at[pl.ds(0, N_CTX - 1)], 9)
        pairs = akv[...].astype(F32)
        scores = dot_t(pairs[:, 0, :].astype(BF16), queries)
        token = lax.broadcasted_iota(jnp.int32, (QTOK, GROUP * QTOK), 1) // GROUP
        seen = lax.broadcasted_iota(jnp.int32, (QTOK, GROUP * QTOK), 0) <= token
        scores = jnp.where(seen, scores, -jnp.inf)
        both = jnp.maximum(peak, jnp.max(scores, axis=0, keepdims=True))
        rescale = jnp.exp2((peak - both) * C2)
        probs = jnp.exp2((scores - both) * C2)
        weight_sum = weight_sum * rescale + jnp.sum(probs, axis=0, keepdims=True)
        mixed = mixed * rescale + jnp.dot(
            pairs[:, 1, :].T.astype(BF16), probs.astype(BF16), preferred_element_type=F32
        )
        return both, weight_sum, mixed

    def local_peers():
        for d in range(1, 16):
            to_z, to_rank = (z_lo + d // 4) % 4, (rank + d) % 4
            yield 4 * to_z + to_rank, ctx_at(to_rank // 2, 4 * z_hi + to_z, to_rank % 2)

    def answer_part():
        arrived(q_all.at[pl.ds(0, N_CTX - 1)], 8)
        queries = q_all[...].astype(F32).reshape(GROUP * QTOK, HD).astype(BF16)
        scores = dot_t(own_k[...], queries)
        peak = jnp.max(scores, axis=0, keepdims=True)
        probs = jnp.exp2((scores - peak) * C2)
        weight_sum = jnp.sum(probs, axis=0, keepdims=True)
        mixed = jnp.dot(own_vt[...], probs.astype(BF16), preferred_element_type=F32)
        peak, weight_sum, mixed = lax.cond(
            c == 0,
            lambda: answer_self(queries, peak, weight_sum, mixed),
            lambda: (peak, weight_sum, mixed),
        )
        l_src[...] = peak * C2 + jnp.log2(weight_sum)
        o_src[...] = (mixed / weight_sum).T.astype(BF16).reshape(16, 16, HD)
        for to, device in local_peers():
            send(o_src.at[to], o_recv.at[local], 10, ctx=device)
            send(l_src, l_recv.at[local], 11, ctx=device)
        o_recv[local] = o_src[local]
        l_recv[local] = l_src[...]

    def merged(parts, levels, first_lane):
        width = levels[0].shape[1]
        row = lax.broadcasted_iota(jnp.int32, (16, width), 0) + first_lane
        mine = lax.broadcasted_iota(jnp.int32, (16, width), 1) == row
        columns = [
            jnp.sum(jnp.where(mine, level, 0.0), axis=1, keepdims=True) for level in levels
        ]
        peak = functools.reduce(jnp.maximum, columns)
        weights = [jnp.exp2(column - peak) for column in columns]
        weight_sum = functools.reduce(jnp.add, weights)
        mixed = functools.reduce(
            jnp.add, [part.astype(F32) * weight for part, weight in zip(parts, weights)]
        )
        return mixed / weight_sum, peak + jnp.log2(weight_sum)

    def answer_local():
        arrived(o_recv.at[pl.ds(0, 15)], 10)
        arrived(l_recv.at[pl.ds(0, 15)], 11)
        mixed, level = merged(
            [o_recv[n] for n in range(16)], [l_recv[n] for n in range(16)], 16 * local
        )
        o2_src[...] = mixed.astype(BF16)
        row = lax.broadcasted_iota(jnp.int32, (16, HD), 0)
        lane = lax.broadcasted_iota(jnp.int32, (16, HD), 1)
        l2_src[...] = jnp.sum(jnp.where(row == lane, level, 0.0), axis=0, keepdims=True)
        for d in range(1, 4):
            to = ctx_at(y, 4 * ((z_hi + d) % 4) + z_lo, k)
            send(o2_src, o2_recv.at[z_hi], 12, ctx=to)
            send(l2_src, l2_recv.at[z_hi], 13, ctx=to)
        o2_recv[z_hi] = o2_src[...]
        l2_recv[z_hi] = l2_src[...]

    def answer_heads():
        arrived(o2_recv.at[pl.ds(0, 3)], 12)
        arrived(l2_recv.at[pl.ds(0, 3)], 13)
        mixed, _ = merged([o2_recv[n] for n in range(4)], [l2_recv[n] for n in range(4)], 0)
        h_src[...] = mixed.astype(BF16)
        for _, device in local_peers():
            send(h_src, h_all.at[local], 14, ctx=device)
        h_all[local] = h_src[...]

    def answer_project():
        arrived(h_all.at[pl.ds(0, 15)], 14)
        h_f[...] = h_all[...].reshape(GROUP * QTOK, HD).astype(F32)
        flat = jnp.concatenate(
            [h_f[pl.ds(h, QTOK, stride=GROUP), :] for h in range(GROUP)], axis=1
        ).astype(BF16)
        share = jnp.dot(flat, w_v[...], preferred_element_type=F32)
        p_src[...] = share.reshape(N_TP, QTOK // N_TP, HD)
        for d in range(1, N_TP):
            to = (p + d) % N_TP
            send(p_src.at[to], p_recv.at[p], 15, tp=to)
        p_recv[p] = p_src[p]

    def answer_sum():
        arrived(p_recv.at[pl.ds(0, N_TP - 1)], 15)
        ans_ref[...] = jnp.sum(p_recv[...], axis=0).astype(BF16)

    for d in range(1, N_CTX):
        send(aq_hbm.at[0], q_all.at[c], 8, ctx=(c + d) % N_CTX)
    near_scatter(0)
    near_scatter(1)

    @pl.when(c != 0)
    def _():
        send(ap_hbm.at[0], akv.at[c], 9, ctx=0)

    @pl.when(c == 0)
    def _():
        own = pltpu.make_async_copy(ap_hbm.at[0], akv.at[0], load_sem.at[4])
        own.start()
        own.wait()

    loads[0].wait()
    pairs_f[...] = pairs_v[...].reshape(2 * BLOCK, HD).astype(F32)
    own_k[...] = pairs_f[pl.ds(0, BLOCK, stride=2), :].astype(BF16)
    own_vt[...] = pairs_f[pl.ds(1, BLOCK, stride=2), :].astype(BF16).T
    loads[1].wait()
    loads[3].wait()
    own_part(0)
    own_part(1)
    own_part(2)
    z_scatter(0)
    own_part(3)
    z_scatter(1)
    answer_part()
    z_gather(0)
    z_gather(1)
    answer_local()
    near_gather(0)
    near_gather(1)
    answer_heads()
    far_here(0)
    far_part(range(4), False)
    far_here(1)
    far_part(range(2), True)
    loads[2].wait()
    answer_project()
    far_part(range(2, 4), True)
    answer_sum()

    for half in range(2):
        sent(cand[half].at[pl.ds(0, 3)], half)
        sent(z_cand[half].at[pl.ds(0, N_Z - 1)], 2 + half)
        sent(far[half].at[0, pl.ds(0, N_Z - 1)], 4 + half)
        sent(far[half].at[pl.ds(0, 3)], 6 + half)
    sent(q_all.at[pl.ds(0, N_CTX - 1)], 8)

    @pl.when(c != 0)
    def _():
        sent(akv.at[0], 9)

    sent(o_recv.at[pl.ds(0, 15)], 10)
    sent(l_recv.at[pl.ds(0, 15)], 11)
    sent(o2_recv.at[pl.ds(0, 3)], 12)
    sent(l2_recv.at[pl.ds(0, 3)], 13)
    sent(h_all.at[pl.ds(0, 15)], 14)
    sent(p_recv.at[pl.ds(0, N_TP - 1)], 15)


def in_hbm(array):
    return pltpu.with_memory_space_constraint(array, pltpu.HBM)


def on_device(
    context_query, context_pairs, anchor_block, answer_query, answer_pairs, output_weight
):
    hbm = pl.BlockSpec(memory_space=pltpu.HBM)
    vmem = pl.BlockSpec(memory_space=pltpu.VMEM)
    out, answer_output = pl.pallas_call(
        kernel,
        out_shape=(
            jax.ShapeDtypeStruct((ROWS, HD), BF16),
            jax.ShapeDtypeStruct((QTOK // N_TP, HD), BF16),
        ),
        in_specs=[pl.BlockSpec(memory_space=pltpu.SMEM), hbm, hbm, hbm, hbm, hbm],
        out_specs=(vmem, vmem),
        scratch_shapes=[
            pltpu.VMEM((ROWS, HD), BF16),
            pltpu.VMEM((4, 2, N_Z, 16, HD), BF16),
            pltpu.VMEM((2 * BLOCK, HD), F32),
            pltpu.VMEM((GROUP * HD, HD), BF16),
            pltpu.VMEM((BLOCK, HD), BF16),
            pltpu.VMEM((HD, BLOCK), BF16),
            pltpu.VMEM((4, N_Z, 16, HD), BF16),
            pltpu.VMEM((4, N_Z, 16, HD), BF16),
            pltpu.VMEM((2, N_Z, 16, HD), BF16),
            pltpu.VMEM((N_Z, 16, HD), BF16),
            pltpu.VMEM((N_Z, 16, HD), BF16),
            pltpu.VMEM((4, N_Z, 16, HD), BF16),
            pltpu.VMEM((4, N_Z, 16, HD), BF16),
            pltpu.VMEM((BLOCK, HD), F32),
            pltpu.VMEM((BLOCK // 2, HD), BF16),
            pltpu.VMEM((HD, BLOCK // 2), BF16),
            pltpu.VMEM((1, ROWS), F32),
            pltpu.VMEM((1, ROWS), F32),
            pltpu.VMEM((HD, ROWS), F32),
            pltpu.VMEM((N_CTX, GROUP, HD), BF16),
            pltpu.VMEM((N_CTX, 2, HD), BF16),
            pltpu.VMEM((16, 16, HD), BF16),
            pltpu.VMEM((1, GROUP * QTOK), F32),
            pltpu.VMEM((16, 16, HD), BF16),
            pltpu.VMEM((16, 1, GROUP * QTOK), F32),
            pltpu.VMEM((16, HD), BF16),
            pltpu.VMEM((1, HD), F32),
            pltpu.VMEM((4, 16, HD), BF16),
            pltpu.VMEM((4, 1, HD), F32),
            pltpu.VMEM((16, HD), BF16),
            pltpu.VMEM((16, 16, HD), BF16),
            pltpu.VMEM((GROUP * QTOK, HD), F32),
            pltpu.VMEM((N_TP, QTOK // N_TP, HD), F32),
            pltpu.VMEM((N_TP, QTOK // N_TP, HD), F32),
            pltpu.SemaphoreType.DMA((5,)),
            pltpu.SemaphoreType.DMA((16,)),
            pltpu.SemaphoreType.DMA((16,)),
        ],
        compiler_params=pltpu.CompilerParams(
            collective_id=0, has_side_effects=True, vmem_limit_bytes=40 * 1024 * 1024
        ),
        cost_estimate=pl.CostEstimate(
            flops=4 * ROWS * BLOCK * HD * 2, bytes_accessed=1 << 22, transcendentals=2 * ROWS * BLOCK
        ),
        name="two_phase_attention",
    )(
        anchor_block,
        in_hbm(context_query.reshape(ROWS, HD)),
        in_hbm(context_pairs.reshape(4, 2, N_Z, 16, HD)),
        in_hbm(answer_query),
        in_hbm(answer_pairs.reshape(1, 2, HD)),
        in_hbm(output_weight),
    )
    return out.reshape(BLOCK, GROUP, HD), answer_output


def solution(mesh):
    in_specs = (
        P("ctx", "tp", None),
        P("ctx", "tp", None, None),
        P(),
        P("ctx", "tp", None),
        P("ctx", "tp", None, None),
        P("tp", "ctx"),
    )
    out_specs = (P("ctx", "tp", None), P("tp", "ctx"))
    return jax.shard_map(
        on_device, mesh=mesh, in_specs=in_specs, out_specs=out_specs, check_vma=False
    )
```

```python
import functools
import math

import jax
import jax.numpy as jnp
from jax import lax
from jax.experimental import pallas as pl
from jax.experimental.pallas import tpu as pltpu
from jax.sharding import PartitionSpec as P

MESH = pl.DeviceIdType.MESH
N_CTX, N_TP, N_Z = 64, 8, 16
HD, GROUP, BLOCK, QTOK = 128, 4, 1024, 64
ROWS = BLOCK * GROUP
COLS = 1024
F32, BF16 = jnp.float32, jnp.bfloat16
C2 = HD**-0.5 * math.log2(math.e)


def dot_t(a, b):
    return lax.dot_general(a, b, (((1,), (1,)), ((), ())), preferred_element_type=F32)


def kernel(
    anchor_ref, q_hbm, pairs_hbm, aq_hbm, ap_hbm, w_hbm,
    out_ref, ans_ref,
    q_v, pairs_v, pairs_f, w_v, own_k, own_vt,
    cand_0, cand_1, z_src, z_cand_0, z_cand_1, far_0, far_1, far_f, far_k, far_vt,
    m_s, l_s, acc_s,
    q_all, akv, o_src, l_src, o_recv, l_recv,
    o2_src, l2_src, o2_recv, l2_recv, h_src, h_all, h_f, p_src, p_recv,
    here_sem, load_sem, send_sem, recv_sem,
):
    c = lax.axis_index("ctx")
    p = lax.axis_index("tp")
    y, z, k = c // 32, (c // 2) % N_Z, c % 2
    rank = 2 * y + k
    z_hi, z_lo = z // 4, z % 4
    local = 4 * z_lo + rank

    def ctx_at(y, z, k):
        return (y * N_Z + z) * 2 + k

    def signal(sem, **device):
        pl.semaphore_signal(sem, inc=1, device_id=device, device_id_type=MESH)

    def signal_z(sem, distance):
        signal(sem, ctx=ctx_at(y, (z + distance) % N_Z, k))
        signal(sem, ctx=ctx_at(y, (z + N_Z - distance) % N_Z, k))

    anchor = anchor_ref[0]
    a_rank, a_z = 2 * (anchor // 32) + anchor % 2, (anchor // 2) % N_Z
    is_anchor = anchor == c

    near = [(y, 1 - k), (1 - y, k), (1 - y, 1 - k)]
    barrier = pltpu.get_barrier_semaphore()
    for to_y, to_k in near:
        signal(barrier, ctx=ctx_at(to_y, z, to_k))
    signal_z(barrier, 1)
    for d in range(1, N_TP):
        signal(barrier, tp=(p + d) % N_TP)
    loads = [
        pltpu.make_async_copy(pairs_hbm, pairs_v, load_sem.at[0]),
        pltpu.make_async_copy(q_hbm, q_v, load_sem.at[1]),
        pltpu.make_async_copy(w_hbm, w_v, load_sem.at[2]),
        pltpu.make_async_copy(aq_hbm.at[0], q_all.at[c], load_sem.at[3]),
        pltpu.make_async_copy(ap_hbm.at[0], akv.at[c], load_sem.at[4]),
    ]
    for load in loads:
        load.start()
    pl.semaphore_wait(barrier, 3 + 2 + N_TP - 1)

    def send(src, dst, sem, **device):
        pltpu.make_async_remote_copy(
            src_ref=src, dst_ref=dst, send_sem=send_sem.at[sem], recv_sem=recv_sem.at[sem],
            device_id=device, device_id_type=MESH,
        ).start()

    def arrived(ref, sem):
        pltpu.make_async_copy(ref, ref, recv_sem.at[sem]).wait()

    def sent(ref, sem):
        pltpu.make_async_copy(ref, ref, send_sem.at[sem]).wait()

    cand, z_cand, far = (cand_0, cand_1), (z_cand_0, z_cand_1), (far_0, far_1)

    def near_scatter(half):
        for to_y, to_k in near:
            to = 2 * to_y + to_k
            send(pairs_hbm.at[to, half], cand[half].at[rank], half, ctx=ctx_at(to_y, z, to_k))

    def z_scatter(half):
        cand[half][rank] = pairs_v[rank, half]
        arrived(cand[half].at[pl.ds(0, 3)], half)
        z_src[half] = cand[half][a_rank]
        for d in range(1, N_Z):
            to = (z + d) % N_Z
            send(z_src.at[half, to], z_cand[half].at[z], 2 + half, ctx=ctx_at(y, to, k))
        z_cand[half][z] = z_src[half, z]

    def z_gather(half):
        arrived(z_cand[half].at[pl.ds(0, N_Z - 1)], 2 + half)
        far[half][rank, z] = z_cand[half][a_z]
        for d in range(1, N_Z):
            to = (z + d) % N_Z
            send(far[half].at[rank, z], far[half].at[rank, z], 4 + half, ctx=ctx_at(y, to, k))

    def near_gather(half):
        arrived(far[half].at[0, pl.ds(0, N_Z - 1)], 4 + half)
        for to_y, to_k in near:
            send(far[half].at[rank], far[half].at[rank], 6 + half, ctx=ctx_at(to_y, z, to_k))

    def own_part(i):
        cols = slice(i * COLS, (i + 1) * COLS)
        scores = dot_t(own_k[0 : (i + 1) * 256, :], q_v[cols, :])
        token = lax.broadcasted_iota(jnp.int32, (256, COLS), 1) // GROUP
        seen = lax.broadcasted_iota(jnp.int32, (256, COLS), 0) <= token
        last = jnp.where(seen, scores[i * 256 :], -jnp.inf)
        scores = jnp.concatenate([scores[: i * 256], last], axis=0) if i else last
        peak = jnp.max(scores, axis=0, keepdims=True)
        probs = jnp.exp2((scores - peak) * C2)
        m_s[:, cols] = peak
        l_s[:, cols] = jnp.sum(probs, axis=0, keepdims=True)
        acc_s[:, cols] = jnp.dot(
            own_vt[:, 0 : (i + 1) * 256], probs.astype(BF16), preferred_element_type=F32
        )

    def far_here(half):
        arrived(far[half].at[pl.ds(0, 3)], 6 + half)
        far_f[...] = far[half][...].reshape(BLOCK, HD).astype(F32)
        far_k[...] = far_f[pl.ds(0, BLOCK // 2, stride=2), :].astype(BF16)
        far_vt[...] = far_f[pl.ds(1, BLOCK // 2, stride=2), :].astype(BF16).T

    def far_part(blocks, last):
        far_weight = jnp.where(is_anchor, 0.0, 1.0).astype(F32)
        for i in blocks:
            cols = slice(i * COLS, (i + 1) * COLS)
            scores = dot_t(far_k[...], q_v[cols, :])
            before = m_s[:, cols]
            peak = jnp.maximum(before, jnp.max(scores, axis=0, keepdims=True))
            probs = jnp.exp2((scores - peak) * C2)
            rescale = jnp.where(is_anchor, 1.0, jnp.exp2((before - peak) * C2))
            weight_sum = l_s[:, cols] * rescale + far_weight * jnp.sum(probs, axis=0, keepdims=True)
            mixed = acc_s[:, cols] * rescale + far_weight * jnp.dot(
                far_vt[...], probs.astype(BF16), preferred_element_type=F32
            )
            if last:
                out_ref[cols, :] = (mixed / weight_sum).T.astype(BF16)
            else:
                m_s[:, cols] = peak
                l_s[:, cols] = weight_sum
                acc_s[:, cols] = mixed


    def answer_self(queries, peak, weight_sum, mixed):
        arrived(akv.at[pl.ds(0, 4 * (N_Z - 1))], 9)
        pairs = akv[...].astype(F32)
        scores = dot_t(pairs[:, 0, :].astype(BF16), queries)
        token = lax.broadcasted_iota(jnp.int32, (QTOK, GROUP * QTOK), 1) // GROUP
        seen = lax.broadcasted_iota(jnp.int32, (QTOK, GROUP * QTOK), 0) <= token
        scores = jnp.where(seen, scores, -jnp.inf)
        both = jnp.maximum(peak, jnp.max(scores, axis=0, keepdims=True))
        rescale = jnp.exp2((peak - both) * C2)
        probs = jnp.exp2((scores - both) * C2)
        weight_sum = weight_sum * rescale + jnp.sum(probs, axis=0, keepdims=True)
        mixed = mixed * rescale + jnp.dot(
            pairs[:, 1, :].T.astype(BF16), probs.astype(BF16), preferred_element_type=F32
        )
        return both, weight_sum, mixed

    def local_peers():
        for d in range(1, 16):
            to_z, to_rank = (z_lo + d // 4) % 4, (rank + d) % 4
            yield 4 * to_z + to_rank, ctx_at(to_rank // 2, 4 * z_hi + to_z, to_rank % 2)

    def answer_near():
        for to_y, to_k in near:
            to = ctx_at(to_y, z, to_k)
            send(aq_hbm.at[0], q_all.at[c], 16, ctx=to)
            send(ap_hbm.at[0], akv.at[c], 17, ctx=to)

    def answer_gather():
        loads[3].wait()
        loads[4].wait()
        arrived(q_all.at[pl.ds(0, 3)], 16)
        arrived(akv.at[pl.ds(0, 3)], 17)
        tokens = [pl.ds(2 * z, 2), pl.ds(2 * (N_Z + z), 2)]
        for d in range(1, N_Z):
            to = ctx_at(y, (z + d) % N_Z, k)
            for two in tokens:
                send(q_all.at[two], q_all.at[two], 8, ctx=to)

        @pl.when((rank == 0) & (z != 0))
        def _():
            for two in tokens:
                send(akv.at[two], akv.at[two], 9, ctx=0)

    def answer_part():
        arrived(q_all.at[pl.ds(0, 4 * (N_Z - 1))], 8)
        queries = q_all[...].astype(F32).reshape(GROUP * QTOK, HD).astype(BF16)
        scores = dot_t(own_k[...], queries)
        peak = jnp.max(scores, axis=0, keepdims=True)
        probs = jnp.exp2((scores - peak) * C2)
        weight_sum = jnp.sum(probs, axis=0, keepdims=True)
        mixed = jnp.dot(own_vt[...], probs.astype(BF16), preferred_element_type=F32)
        peak, weight_sum, mixed = lax.cond(
            c == 0,
            lambda: answer_self(queries, peak, weight_sum, mixed),
            lambda: (peak, weight_sum, mixed),
        )
        l_src[...] = peak * C2 + jnp.log2(weight_sum)
        o_src[...] = (mixed / weight_sum).T.astype(BF16).reshape(16, 16, HD)
        for to, device in local_peers():
            send(o_src.at[to], o_recv.at[local], 10, ctx=device)
            send(l_src, l_recv.at[local], 11, ctx=device)
        o_recv[local] = o_src[local]
        l_recv[local] = l_src[...]

    def merged(parts, levels, first_lane):
        width = levels[0].shape[1]
        row = lax.broadcasted_iota(jnp.int32, (16, width), 0) + first_lane
        mine = lax.broadcasted_iota(jnp.int32, (16, width), 1) == row
        columns = [
            jnp.sum(jnp.where(mine, level, 0.0), axis=1, keepdims=True) for level in levels
        ]
        peak = functools.reduce(jnp.maximum, columns)
        weights = [jnp.exp2(column - peak) for column in columns]
        weight_sum = functools.reduce(jnp.add, weights)
        mixed = functools.reduce(
            jnp.add, [part.astype(F32) * weight for part, weight in zip(parts, weights)]
        )
        return mixed / weight_sum, peak + jnp.log2(weight_sum)

    def answer_local():
        arrived(o_recv.at[pl.ds(0, 15)], 10)
        arrived(l_recv.at[pl.ds(0, 15)], 11)
        mixed, level = merged(
            [o_recv[n] for n in range(16)], [l_recv[n] for n in range(16)], 16 * local
        )
        o2_src[...] = mixed.astype(BF16)
        row = lax.broadcasted_iota(jnp.int32, (16, HD), 0)
        lane = lax.broadcasted_iota(jnp.int32, (16, HD), 1)
        l2_src[...] = jnp.sum(jnp.where(row == lane, level, 0.0), axis=0, keepdims=True)
        for d in range(1, 4):
            to = ctx_at(y, 4 * ((z_hi + d) % 4) + z_lo, k)
            send(o2_src, o2_recv.at[z_hi], 12, ctx=to)
            send(l2_src, l2_recv.at[z_hi], 13, ctx=to)
        o2_recv[z_hi] = o2_src[...]
        l2_recv[z_hi] = l2_src[...]

    def answer_heads():
        arrived(o2_recv.at[pl.ds(0, 3)], 12)
        arrived(l2_recv.at[pl.ds(0, 3)], 13)
        mixed, _ = merged([o2_recv[n] for n in range(4)], [l2_recv[n] for n in range(4)], 0)
        h_src[...] = mixed.astype(BF16)
        for _, device in local_peers():
            send(h_src, h_all.at[local], 14, ctx=device)
        h_all[local] = h_src[...]

    def answer_project():
        arrived(h_all.at[pl.ds(0, 15)], 14)
        h_f[...] = h_all[...].reshape(GROUP * QTOK, HD).astype(F32)
        flat = jnp.concatenate(
            [h_f[pl.ds(h, QTOK, stride=GROUP), :] for h in range(GROUP)], axis=1
        ).astype(BF16)
        share = jnp.dot(flat, w_v[...], preferred_element_type=F32)
        p_src[...] = share.reshape(N_TP, QTOK // N_TP, HD)
        for d in range(1, N_TP):
            to = (p + d) % N_TP
            send(p_src.at[to], p_recv.at[p], 15, tp=to)
        p_recv[p] = p_src[p]

    def answer_sum():
        arrived(p_recv.at[pl.ds(0, N_TP - 1)], 15)
        ans_ref[...] = jnp.sum(p_recv[...], axis=0).astype(BF16)

    near_scatter(0)
    signal_z(here_sem.at[0], 1)
    answer_near()
    near_scatter(1)
    loads[0].wait()
    pairs_f[...] = pairs_v[...].reshape(2 * BLOCK, HD).astype(F32)
    own_k[...] = pairs_f[pl.ds(0, BLOCK, stride=2), :].astype(BF16)
    own_vt[...] = pairs_f[pl.ds(1, BLOCK, stride=2), :].astype(BF16).T
    loads[1].wait()
    pl.semaphore_wait(here_sem.at[0], 2)
    signal_z(here_sem.at[1], 2)
    own_part(0)
    own_part(1)
    pl.semaphore_wait(here_sem.at[1], 2)
    signal_z(here_sem.at[2], 4)
    own_part(2)
    pl.semaphore_wait(here_sem.at[2], 2)
    answer_gather()
    z_scatter(0)
    own_part(3)
    z_scatter(1)
    answer_part()
    z_gather(0)
    z_gather(1)
    answer_local()
    near_gather(0)
    near_gather(1)
    answer_heads()
    far_here(0)
    far_part(range(4), False)
    far_here(1)
    far_part(range(2), True)
    loads[2].wait()
    answer_project()
    far_part(range(2, 4), True)
    answer_sum()

    for half in range(2):
        sent(cand[half].at[pl.ds(0, 3)], half)
        sent(z_cand[half].at[pl.ds(0, N_Z - 1)], 2 + half)
        sent(far[half].at[0, pl.ds(0, N_Z - 1)], 4 + half)
        sent(far[half].at[pl.ds(0, 3)], 6 + half)
    sent(q_all.at[pl.ds(0, 3)], 16)
    sent(akv.at[pl.ds(0, 3)], 17)
    sent(q_all.at[pl.ds(0, 4 * (N_Z - 1))], 8)

    @pl.when((rank == 0) & (z != 0))
    def _():
        sent(akv.at[pl.ds(0, 4)], 9)

    sent(o_recv.at[pl.ds(0, 15)], 10)
    sent(l_recv.at[pl.ds(0, 15)], 11)
    sent(o2_recv.at[pl.ds(0, 3)], 12)
    sent(l2_recv.at[pl.ds(0, 3)], 13)
    sent(h_all.at[pl.ds(0, 15)], 14)
    sent(p_recv.at[pl.ds(0, N_TP - 1)], 15)


def in_hbm(array):
    return pltpu.with_memory_space_constraint(array, pltpu.HBM)


def on_device(
    context_query, context_pairs, anchor_block, answer_query, answer_pairs, output_weight
):
    hbm = pl.BlockSpec(memory_space=pltpu.HBM)
    vmem = pl.BlockSpec(memory_space=pltpu.VMEM)
    out, answer_output = pl.pallas_call(
        kernel,
        out_shape=(
            jax.ShapeDtypeStruct((ROWS, HD), BF16),
            jax.ShapeDtypeStruct((QTOK // N_TP, HD), BF16),
        ),
        in_specs=[pl.BlockSpec(memory_space=pltpu.SMEM), hbm, hbm, hbm, hbm, hbm],
        out_specs=(vmem, vmem),
        scratch_shapes=[
            pltpu.VMEM((ROWS, HD), BF16),
            pltpu.VMEM((4, 2, N_Z, 16, HD), BF16),
            pltpu.VMEM((2 * BLOCK, HD), F32),
            pltpu.VMEM((GROUP * HD, HD), BF16),
            pltpu.VMEM((BLOCK, HD), BF16),
            pltpu.VMEM((HD, BLOCK), BF16),
            pltpu.VMEM((4, N_Z, 16, HD), BF16),
            pltpu.VMEM((4, N_Z, 16, HD), BF16),
            pltpu.VMEM((2, N_Z, 16, HD), BF16),
            pltpu.VMEM((N_Z, 16, HD), BF16),
            pltpu.VMEM((N_Z, 16, HD), BF16),
            pltpu.VMEM((4, N_Z, 16, HD), BF16),
            pltpu.VMEM((4, N_Z, 16, HD), BF16),
            pltpu.VMEM((BLOCK, HD), F32),
            pltpu.VMEM((BLOCK // 2, HD), BF16),
            pltpu.VMEM((HD, BLOCK // 2), BF16),
            pltpu.VMEM((1, ROWS), F32),
            pltpu.VMEM((1, ROWS), F32),
            pltpu.VMEM((HD, ROWS), F32),
            pltpu.VMEM((N_CTX, GROUP, HD), BF16),
            pltpu.VMEM((N_CTX, 2, HD), BF16),
            pltpu.VMEM((16, 16, HD), BF16),
            pltpu.VMEM((1, GROUP * QTOK), F32),
            pltpu.VMEM((16, 16, HD), BF16),
            pltpu.VMEM((16, 1, GROUP * QTOK), F32),
            pltpu.VMEM((16, HD), BF16),
            pltpu.VMEM((1, HD), F32),
            pltpu.VMEM((4, 16, HD), BF16),
            pltpu.VMEM((4, 1, HD), F32),
            pltpu.VMEM((16, HD), BF16),
            pltpu.VMEM((16, 16, HD), BF16),
            pltpu.VMEM((GROUP * QTOK, HD), F32),
            pltpu.VMEM((N_TP, QTOK // N_TP, HD), F32),
            pltpu.VMEM((N_TP, QTOK // N_TP, HD), F32),
            pltpu.SemaphoreType.REGULAR((3,)),
            pltpu.SemaphoreType.DMA((5,)),
            pltpu.SemaphoreType.DMA((18,)),
            pltpu.SemaphoreType.DMA((18,)),
        ],
        compiler_params=pltpu.CompilerParams(
            collective_id=0, has_side_effects=True, vmem_limit_bytes=40 * 1024 * 1024
        ),
        cost_estimate=pl.CostEstimate(
            flops=4 * ROWS * BLOCK * HD * 2, bytes_accessed=1 << 22, transcendentals=2 * ROWS * BLOCK
        ),
        name="two_phase_attention",
    )(
        anchor_block,
        in_hbm(context_query.reshape(ROWS, HD)),
        in_hbm(context_pairs.reshape(4, 2, N_Z, 16, HD)),
        in_hbm(answer_query),
        in_hbm(answer_pairs.reshape(1, 2, HD)),
        in_hbm(output_weight),
    )
    return out.reshape(BLOCK, GROUP, HD), answer_output


def solution(mesh):
    in_specs = (
        P("ctx", "tp", None),
        P("ctx", "tp", None, None),
        P(),
        P("ctx", "tp", None),
        P("ctx", "tp", None, None),
        P("tp", "ctx"),
    )
    out_specs = (P("ctx", "tp", None), P("tp", "ctx"))
    return jax.shard_map(
        on_device, mesh=mesh, in_specs=in_specs, out_specs=out_specs, check_vma=False
    )
```

```python
import functools
import math

import jax
import jax.numpy as jnp
from jax import lax
from jax.experimental import pallas as pl
from jax.experimental.pallas import tpu as pltpu
from jax.sharding import PartitionSpec as P

MESH = pl.DeviceIdType.MESH
N_CTX, N_TP, N_Z = 64, 8, 16
HD, GROUP, BLOCK, QTOK = 128, 4, 1024, 64
ROWS = BLOCK * GROUP
COLS = 1024
F32, BF16 = jnp.float32, jnp.bfloat16
C2 = HD**-0.5 * math.log2(math.e)


def dot_t(a, b):
    return lax.dot_general(a, b, (((1,), (1,)), ((), ())), preferred_element_type=F32)


def kernel(
    anchor_ref, q_hbm, pairs_hbm, aq_hbm, ap_hbm, w_hbm,
    out_ref, ans_ref,
    q_v, pairs_v, pairs_f, w_v, own_k, own_vt,
    cand_0, cand_1, z_src, z_cand_0, z_cand_1, far_0, far_1, far_f, far_k, far_vt,
    m_s, l_s, acc_s,
    q_all, akv, o_src, l_src, o_recv, l_recv,
    o2_src, l2_src, o2_recv, l2_recv, h_src, h_all, h_f, p_src, p_recv,
    here_sem, load_sem, send_sem, recv_sem,
):
    c = lax.axis_index("ctx")
    p = lax.axis_index("tp")
    y, z, k = c // 32, (c // 2) % N_Z, c % 2
    rank = 2 * y + k
    z_hi, z_lo = z // 4, z % 4
    local = 4 * z_lo + rank

    def ctx_at(y, z, k):
        return (y * N_Z + z) * 2 + k

    def signal(sem, **device):
        pl.semaphore_signal(sem, inc=1, device_id=device, device_id_type=MESH)

    def signal_z(sem, distance):
        signal(sem, ctx=ctx_at(y, (z + distance) % N_Z, k))
        signal(sem, ctx=ctx_at(y, (z + N_Z - distance) % N_Z, k))

    anchor = anchor_ref[0]
    a_rank, a_z = 2 * (anchor // 32) + anchor % 2, (anchor // 2) % N_Z
    is_anchor = anchor == c

    near = [(y, 1 - k), (1 - y, k), (1 - y, 1 - k)]
    barrier = pltpu.get_barrier_semaphore()
    for to_y, to_k in near:
        signal(barrier, ctx=ctx_at(to_y, z, to_k))
    for distance in (1, 2):
        signal_z(barrier, distance)
    for d in range(1, N_TP):
        signal(barrier, tp=(p + d) % N_TP)
    loads = [
        pltpu.make_async_copy(pairs_hbm, pairs_v, load_sem.at[0]),
        pltpu.make_async_copy(q_hbm, q_v, load_sem.at[1]),
        pltpu.make_async_copy(w_hbm, w_v, load_sem.at[2]),
        pltpu.make_async_copy(aq_hbm.at[0], q_all.at[c], load_sem.at[3]),
        pltpu.make_async_copy(ap_hbm.at[0], akv.at[c], load_sem.at[4]),
    ]
    for load in loads:
        load.start()
    pl.semaphore_wait(barrier, 3 + 4 + N_TP - 1)

    def send(src, dst, sem, **device):
        pltpu.make_async_remote_copy(
            src_ref=src, dst_ref=dst, send_sem=send_sem.at[sem], recv_sem=recv_sem.at[sem],
            device_id=device, device_id_type=MESH,
        ).start()

    def arrived(ref, sem):
        pltpu.make_async_copy(ref, ref, recv_sem.at[sem]).wait()

    def sent(ref, sem):
        pltpu.make_async_copy(ref, ref, send_sem.at[sem]).wait()

    cand, z_cand, far = (cand_0, cand_1), (z_cand_0, z_cand_1), (far_0, far_1)

    def near_scatter(half):
        for to_y, to_k in near:
            to = 2 * to_y + to_k
            send(pairs_hbm.at[to, half], cand[half].at[rank], half, ctx=ctx_at(to_y, z, to_k))

    def z_scatter(half):
        cand[half][rank] = pairs_v[rank, half]
        arrived(cand[half].at[pl.ds(0, 3)], half)
        z_src[half] = cand[half][a_rank]
        for d in range(1, N_Z):
            to = (z + d) % N_Z
            send(z_src.at[half, to], z_cand[half].at[z], 2 + half, ctx=ctx_at(y, to, k))
        z_cand[half][z] = z_src[half, z]

    def z_gather(half):
        arrived(z_cand[half].at[pl.ds(0, N_Z - 1)], 2 + half)
        far[half][rank, z] = z_cand[half][a_z]
        for d in range(1, N_Z):
            to = (z + d) % N_Z
            send(far[half].at[rank, z], far[half].at[rank, z], 4 + half, ctx=ctx_at(y, to, k))

    def near_gather(half):
        arrived(far[half].at[0, pl.ds(0, N_Z - 1)], 4 + half)
        for to_y, to_k in near:
            send(far[half].at[rank], far[half].at[rank], 6 + half, ctx=ctx_at(to_y, z, to_k))

    def own_part(i):
        cols = slice(i * COLS, (i + 1) * COLS)
        scores = dot_t(own_k[0 : (i + 1) * 256, :], q_v[cols, :])
        token = lax.broadcasted_iota(jnp.int32, (256, COLS), 1) // GROUP
        seen = lax.broadcasted_iota(jnp.int32, (256, COLS), 0) <= token
        last = jnp.where(seen, scores[i * 256 :], -jnp.inf)
        scores = jnp.concatenate([scores[: i * 256], last], axis=0) if i else last
        peak = jnp.max(scores, axis=0, keepdims=True)
        probs = jnp.exp2((scores - peak) * C2)
        m_s[:, cols] = peak
        l_s[:, cols] = jnp.sum(probs, axis=0, keepdims=True)
        acc_s[:, cols] = jnp.dot(
            own_vt[:, 0 : (i + 1) * 256], probs.astype(BF16), preferred_element_type=F32
        )

    def far_here(half):
        arrived(far[half].at[pl.ds(0, 3)], 6 + half)
        far_f[...] = far[half][...].reshape(BLOCK, HD).astype(F32)
        far_k[...] = far_f[pl.ds(0, BLOCK // 2, stride=2), :].astype(BF16)
        far_vt[...] = far_f[pl.ds(1, BLOCK // 2, stride=2), :].astype(BF16).T

    def far_part(blocks, last):
        for i in blocks:
            cols = slice(i * COLS, (i + 1) * COLS)
            scores = dot_t(far_k[...], q_v[cols, :])
            before = m_s[:, cols]
            peak = jnp.maximum(before, jnp.max(scores, axis=0, keepdims=True))
            probs = jnp.exp2((scores - jnp.where(is_anchor, 1e38, peak)) * C2)
            rescale = jnp.where(is_anchor, 1.0, jnp.exp2((before - peak) * C2))
            weight_sum = l_s[:, cols] * rescale + jnp.sum(probs, axis=0, keepdims=True)
            mixed = acc_s[:, cols] * rescale + jnp.dot(
                far_vt[...], probs.astype(BF16), preferred_element_type=F32
            )
            if last:
                out_ref[cols, :] = (mixed * (1.0 / weight_sum)).T.astype(BF16)
            else:
                m_s[:, cols] = peak
                l_s[:, cols] = weight_sum
                acc_s[:, cols] = mixed


    def answer_self(queries, peak, weight_sum, mixed):
        arrived(akv.at[pl.ds(0, 4 * (N_Z - 1))], 9)
        pairs = akv[...].astype(F32)
        scores = dot_t(pairs[:, 0, :].astype(BF16), queries)
        token = lax.broadcasted_iota(jnp.int32, (QTOK, GROUP * QTOK), 1) // GROUP
        seen = lax.broadcasted_iota(jnp.int32, (QTOK, GROUP * QTOK), 0) <= token
        scores = jnp.where(seen, scores, -jnp.inf)
        both = jnp.maximum(peak, jnp.max(scores, axis=0, keepdims=True))
        rescale = jnp.exp2((peak - both) * C2)
        probs = jnp.exp2((scores - both) * C2)
        weight_sum = weight_sum * rescale + jnp.sum(probs, axis=0, keepdims=True)
        mixed = mixed * rescale + jnp.dot(
            pairs[:, 1, :].T.astype(BF16), probs.astype(BF16), preferred_element_type=F32
        )
        return both, weight_sum, mixed

    def local_peers():
        for d in range(1, 16):
            to_z, to_rank = (z_lo + d // 4) % 4, (rank + d) % 4
            yield 4 * to_z + to_rank, ctx_at(to_rank // 2, 4 * z_hi + to_z, to_rank % 2)

    def answer_near():
        for to_y, to_k in near:
            to = ctx_at(to_y, z, to_k)
            send(aq_hbm.at[0], q_all.at[c], 16, ctx=to)
            send(ap_hbm.at[0], akv.at[c], 17, ctx=to)

    def answer_gather():
        loads[3].wait()
        loads[4].wait()
        arrived(q_all.at[pl.ds(0, 3)], 16)
        arrived(akv.at[pl.ds(0, 3)], 17)
        tokens = [pl.ds(2 * z, 2), pl.ds(2 * (N_Z + z), 2)]
        for d in range(1, N_Z):
            to = ctx_at(y, (z + d) % N_Z, k)
            for two in tokens:
                send(q_all.at[two], q_all.at[two], 8, ctx=to)

        @pl.when((rank == 0) & (z != 0))
        def _():
            for two in tokens:
                send(akv.at[two], akv.at[two], 9, ctx=0)

    def answer_part():
        arrived(q_all.at[pl.ds(0, 4 * (N_Z - 1))], 8)
        queries = q_all[...].astype(F32).reshape(GROUP * QTOK, HD).astype(BF16)
        scores = dot_t(own_k[...], queries)
        peak = jnp.max(scores, axis=0, keepdims=True)
        probs = jnp.exp2((scores - peak) * C2)
        weight_sum = jnp.sum(probs, axis=0, keepdims=True)
        mixed = jnp.dot(own_vt[...], probs.astype(BF16), preferred_element_type=F32)
        peak, weight_sum, mixed = lax.cond(
            c == 0,
            lambda: answer_self(queries, peak, weight_sum, mixed),
            lambda: (peak, weight_sum, mixed),
        )
        l_src[...] = peak * C2 + jnp.log2(weight_sum)
        o_src[...] = (mixed * (1.0 / weight_sum)).T.astype(BF16).reshape(16, 16, HD)
        for to, device in local_peers():
            send(o_src.at[to], o_recv.at[local], 10, ctx=device)
            send(l_src, l_recv.at[local], 11, ctx=device)
        o_recv[local] = o_src[local]
        l_recv[local] = l_src[...]

    def merged(parts, levels, first_lane):
        width = levels[0].shape[1]
        row = lax.broadcasted_iota(jnp.int32, (16, width), 0) + first_lane
        mine = lax.broadcasted_iota(jnp.int32, (16, width), 1) == row
        columns = [
            jnp.sum(jnp.where(mine, level, 0.0), axis=1, keepdims=True) for level in levels
        ]
        peak = functools.reduce(jnp.maximum, columns)
        weights = [jnp.exp2(column - peak) for column in columns]
        weight_sum = functools.reduce(jnp.add, weights)
        mixed = functools.reduce(
            jnp.add, [part.astype(F32) * weight for part, weight in zip(parts, weights)]
        )
        return mixed / weight_sum, peak + jnp.log2(weight_sum)

    def answer_local():
        arrived(o_recv.at[pl.ds(0, 15)], 10)
        arrived(l_recv.at[pl.ds(0, 15)], 11)
        mixed, level = merged(
            [o_recv[n] for n in range(16)], [l_recv[n] for n in range(16)], 16 * local
        )
        o2_src[...] = mixed.astype(BF16)
        row = lax.broadcasted_iota(jnp.int32, (16, HD), 0)
        lane = lax.broadcasted_iota(jnp.int32, (16, HD), 1)
        l2_src[...] = jnp.sum(jnp.where(row == lane, level, 0.0), axis=0, keepdims=True)
        for d in range(1, 4):
            to = ctx_at(y, 4 * ((z_hi + d) % 4) + z_lo, k)
            send(o2_src, o2_recv.at[z_hi], 12, ctx=to)
            send(l2_src, l2_recv.at[z_hi], 13, ctx=to)
        o2_recv[z_hi] = o2_src[...]
        l2_recv[z_hi] = l2_src[...]

    def answer_heads():
        arrived(o2_recv.at[pl.ds(0, 3)], 12)
        arrived(l2_recv.at[pl.ds(0, 3)], 13)
        mixed, _ = merged([o2_recv[n] for n in range(4)], [l2_recv[n] for n in range(4)], 0)
        h_src[...] = mixed.astype(BF16)
        for _, device in local_peers():
            send(h_src, h_all.at[local], 14, ctx=device)
        h_all[local] = h_src[...]

    def answer_project():
        arrived(h_all.at[pl.ds(0, 15)], 14)
        h_f[...] = h_all[...].reshape(GROUP * QTOK, HD).astype(F32)
        flat = jnp.concatenate(
            [h_f[pl.ds(h, QTOK, stride=GROUP), :] for h in range(GROUP)], axis=1
        ).astype(BF16)
        share = jnp.dot(flat, w_v[...], preferred_element_type=F32)
        p_src[...] = share.reshape(N_TP, QTOK // N_TP, HD)
        for d in range(1, N_TP):
            to = (p + d) % N_TP
            send(p_src.at[to], p_recv.at[p], 15, tp=to)
        p_recv[p] = p_src[p]

    def answer_sum():
        arrived(p_recv.at[pl.ds(0, N_TP - 1)], 15)
        ans_ref[...] = jnp.sum(p_recv[...], axis=0).astype(BF16)

    near_scatter(0)
    signal_z(here_sem.at[0], 2)
    answer_near()
    near_scatter(1)
    loads[0].wait()
    pairs_f[...] = pairs_v[...].reshape(2 * BLOCK, HD).astype(F32)
    own_k[...] = pairs_f[pl.ds(0, BLOCK, stride=2), :].astype(BF16)
    own_vt[...] = pairs_f[pl.ds(1, BLOCK, stride=2), :].astype(BF16).T
    loads[1].wait()
    pl.semaphore_wait(here_sem.at[0], 2)
    signal_z(here_sem.at[1], 4)
    own_part(0)
    own_part(1)
    own_part(2)
    pl.semaphore_wait(here_sem.at[1], 2)
    answer_gather()
    z_scatter(0)
    z_scatter(1)
    own_part(3)
    answer_part()
    z_gather(0)
    z_gather(1)
    answer_local()
    near_gather(0)
    near_gather(1)
    answer_heads()
    far_here(0)
    far_part(range(4), False)
    loads[2].wait()
    answer_project()
    far_here(1)
    far_part(range(4), True)
    answer_sum()

    for half in range(2):
        sent(cand[half].at[pl.ds(0, 3)], half)
        sent(z_cand[half].at[pl.ds(0, N_Z - 1)], 2 + half)
        sent(far[half].at[0, pl.ds(0, N_Z - 1)], 4 + half)
        sent(far[half].at[pl.ds(0, 3)], 6 + half)
    sent(q_all.at[pl.ds(0, 3)], 16)
    sent(akv.at[pl.ds(0, 3)], 17)
    sent(q_all.at[pl.ds(0, 4 * (N_Z - 1))], 8)

    @pl.when((rank == 0) & (z != 0))
    def _():
        sent(akv.at[pl.ds(0, 4)], 9)

    sent(o_recv.at[pl.ds(0, 15)], 10)
    sent(l_recv.at[pl.ds(0, 15)], 11)
    sent(o2_recv.at[pl.ds(0, 3)], 12)
    sent(l2_recv.at[pl.ds(0, 3)], 13)
    sent(h_all.at[pl.ds(0, 15)], 14)
    sent(p_recv.at[pl.ds(0, N_TP - 1)], 15)


def in_hbm(array):
    return pltpu.with_memory_space_constraint(array, pltpu.HBM)


def on_device(
    context_query, context_pairs, anchor_block, answer_query, answer_pairs, output_weight
):
    hbm = pl.BlockSpec(memory_space=pltpu.HBM)
    vmem = pl.BlockSpec(memory_space=pltpu.VMEM)
    out, answer_output = pl.pallas_call(
        kernel,
        out_shape=(
            jax.ShapeDtypeStruct((ROWS, HD), BF16),
            jax.ShapeDtypeStruct((QTOK // N_TP, HD), BF16),
        ),
        in_specs=[pl.BlockSpec(memory_space=pltpu.SMEM), hbm, hbm, hbm, hbm, hbm],
        out_specs=(vmem, vmem),
        scratch_shapes=[
            pltpu.VMEM((ROWS, HD), BF16),
            pltpu.VMEM((4, 2, N_Z, 16, HD), BF16),
            pltpu.VMEM((2 * BLOCK, HD), F32),
            pltpu.VMEM((GROUP * HD, HD), BF16),
            pltpu.VMEM((BLOCK, HD), BF16),
            pltpu.VMEM((HD, BLOCK), BF16),
            pltpu.VMEM((4, N_Z, 16, HD), BF16),
            pltpu.VMEM((4, N_Z, 16, HD), BF16),
            pltpu.VMEM((2, N_Z, 16, HD), BF16),
            pltpu.VMEM((N_Z, 16, HD), BF16),
            pltpu.VMEM((N_Z, 16, HD), BF16),
            pltpu.VMEM((4, N_Z, 16, HD), BF16),
            pltpu.VMEM((4, N_Z, 16, HD), BF16),
            pltpu.VMEM((BLOCK, HD), F32),
            pltpu.VMEM((BLOCK // 2, HD), BF16),
            pltpu.VMEM((HD, BLOCK // 2), BF16),
            pltpu.VMEM((1, ROWS), F32),
            pltpu.VMEM((1, ROWS), F32),
            pltpu.VMEM((HD, ROWS), F32),
            pltpu.VMEM((N_CTX, GROUP, HD), BF16),
            pltpu.VMEM((N_CTX, 2, HD), BF16),
            pltpu.VMEM((16, 16, HD), BF16),
            pltpu.VMEM((1, GROUP * QTOK), F32),
            pltpu.VMEM((16, 16, HD), BF16),
            pltpu.VMEM((16, 1, GROUP * QTOK), F32),
            pltpu.VMEM((16, HD), BF16),
            pltpu.VMEM((1, HD), F32),
            pltpu.VMEM((4, 16, HD), BF16),
            pltpu.VMEM((4, 1, HD), F32),
            pltpu.VMEM((16, HD), BF16),
            pltpu.VMEM((16, 16, HD), BF16),
            pltpu.VMEM((GROUP * QTOK, HD), F32),
            pltpu.VMEM((N_TP, QTOK // N_TP, HD), F32),
            pltpu.VMEM((N_TP, QTOK // N_TP, HD), F32),
            pltpu.SemaphoreType.REGULAR((2,)),
            pltpu.SemaphoreType.DMA((5,)),
            pltpu.SemaphoreType.DMA((18,)),
            pltpu.SemaphoreType.DMA((18,)),
        ],
        compiler_params=pltpu.CompilerParams(
            collective_id=0, has_side_effects=True, vmem_limit_bytes=40 * 1024 * 1024
        ),
        cost_estimate=pl.CostEstimate(
            flops=4 * ROWS * BLOCK * HD * 2, bytes_accessed=1 << 22, transcendentals=2 * ROWS * BLOCK
        ),
        name="two_phase_attention",
    )(
        anchor_block,
        in_hbm(context_query.reshape(ROWS, HD)),
        in_hbm(context_pairs.reshape(4, 2, N_Z, 16, HD)),
        in_hbm(answer_query),
        in_hbm(answer_pairs.reshape(1, 2, HD)),
        in_hbm(output_weight),
    )
    return out.reshape(BLOCK, GROUP, HD), answer_output


def solution(mesh):
    in_specs = (
        P("ctx", "tp", None),
        P("ctx", "tp", None, None),
        P(),
        P("ctx", "tp", None),
        P("ctx", "tp", None, None),
        P("tp", "ctx"),
    )
    out_specs = (P("ctx", "tp", None), P("tp", "ctx"))
    return jax.shard_map(
        on_device, mesh=mesh, in_specs=in_specs, out_specs=out_specs, check_vma=False
    )
```

```python
import functools
import math

import jax
import jax.numpy as jnp
from jax import lax
from jax.experimental import pallas as pl
from jax.experimental.pallas import tpu as pltpu
from jax.sharding import PartitionSpec as P

MESH = pl.DeviceIdType.MESH
N_CTX, N_TP, N_Z = 64, 8, 16
HD, GROUP, BLOCK, QTOK = 128, 4, 1024, 64
ROWS = BLOCK * GROUP
COLS = 1024
FAR_FIRST = sorted(range(1, N_Z), key=lambda d: abs(d - N_Z // 2))
F32, BF16 = jnp.float32, jnp.bfloat16
C2 = HD**-0.5 * math.log2(math.e)


def dot_t(a, b):
    return lax.dot_general(a, b, (((1,), (1,)), ((), ())), preferred_element_type=F32)


def kernel(
    anchor_ref, q_hbm, pairs_hbm, aq_hbm, ap_hbm, w_hbm,
    out_ref, ans_ref,
    q_v, pairs_v, pairs_f, w_v, own_k, own_vt,
    cand_0, cand_1, z_src, z_cand_0, z_cand_1, far_0, far_1, far_f, far_k, far_vt,
    m_s, l_s, acc_s,
    q_all, akv, o_src, l_src, o_recv, l_recv,
    o2_src, l2_src, o2_recv, l2_recv, h_src, h_all, h_f, p_src, p_recv,
    here_sem, load_sem, send_sem, recv_sem,
):
    c = lax.axis_index("ctx")
    p = lax.axis_index("tp")
    y, z, k = c // 32, (c // 2) % N_Z, c % 2
    rank = 2 * y + k
    z_hi, z_lo = z // 4, z % 4
    local = 4 * z_lo + rank

    def ctx_at(y, z, k):
        return (y * N_Z + z) * 2 + k

    def signal(sem, **device):
        pl.semaphore_signal(sem, inc=1, device_id=device, device_id_type=MESH)

    def signal_z(sem, distance):
        signal(sem, ctx=ctx_at(y, (z + distance) % N_Z, k))
        signal(sem, ctx=ctx_at(y, (z + N_Z - distance) % N_Z, k))

    anchor = anchor_ref[0]
    a_rank, a_z = 2 * (anchor // 32) + anchor % 2, (anchor // 2) % N_Z
    is_anchor = anchor == c

    near = [(1 - y, k), (1 - y, 1 - k), (y, 1 - k)]
    barrier = pltpu.get_barrier_semaphore()
    for to_y, to_k in near:
        signal(barrier, ctx=ctx_at(to_y, z, to_k))
    for distance in (1, 2):
        signal_z(barrier, distance)
    for d in range(1, N_TP):
        signal(barrier, tp=(p + d) % N_TP)
    loads = [
        pltpu.make_async_copy(pairs_hbm, pairs_v, load_sem.at[0]),
        pltpu.make_async_copy(q_hbm, q_v, load_sem.at[1]),
        pltpu.make_async_copy(w_hbm, w_v, load_sem.at[2]),
        pltpu.make_async_copy(aq_hbm.at[0], q_all.at[c], load_sem.at[3]),
        pltpu.make_async_copy(ap_hbm.at[0], akv.at[c], load_sem.at[4]),
    ]
    for load in loads:
        load.start()
    pl.semaphore_wait(barrier, 3 + 4 + N_TP - 1)

    def send(src, dst, sem, **device):
        pltpu.make_async_remote_copy(
            src_ref=src, dst_ref=dst, send_sem=send_sem.at[sem], recv_sem=recv_sem.at[sem],
            device_id=device, device_id_type=MESH,
        ).start()

    def arrived(ref, sem):
        pltpu.make_async_copy(ref, ref, recv_sem.at[sem]).wait()

    def sent(ref, sem):
        pltpu.make_async_copy(ref, ref, send_sem.at[sem]).wait()

    cand, z_cand, far = (cand_0, cand_1), (z_cand_0, z_cand_1), (far_0, far_1)

    def near_scatter(half):
        for to_y, to_k in near:
            to = 2 * to_y + to_k
            send(pairs_hbm.at[to, half], cand[half].at[rank], half, ctx=ctx_at(to_y, z, to_k))

    def z_scatter(half):
        cand[half][rank] = pairs_v[rank, half]
        arrived(cand[half].at[pl.ds(0, 3)], half)
        z_src[half] = cand[half][a_rank]
        for d in FAR_FIRST:
            to = (z + d) % N_Z
            send(z_src.at[half, to], z_cand[half].at[z], 2 + half, ctx=ctx_at(y, to, k))
        z_cand[half][z] = z_src[half, z]

    def z_gather(half):
        arrived(z_cand[half].at[pl.ds(0, N_Z - 1)], 2 + half)
        far[half][rank, z] = z_cand[half][a_z]
        for d in FAR_FIRST:
            to = (z + d) % N_Z
            send(far[half].at[rank, z], far[half].at[rank, z], 4 + half, ctx=ctx_at(y, to, k))

    def near_gather(half):
        arrived(far[half].at[0, pl.ds(0, N_Z - 1)], 4 + half)
        for to_y, to_k in near:
            send(far[half].at[rank], far[half].at[rank], 6 + half, ctx=ctx_at(to_y, z, to_k))

    def own_part(i):
        cols = slice(i * COLS, (i + 1) * COLS)
        scores = dot_t(own_k[0 : (i + 1) * 256, :], q_v[cols, :])
        token = lax.broadcasted_iota(jnp.int32, (256, COLS), 1) // GROUP
        seen = lax.broadcasted_iota(jnp.int32, (256, COLS), 0) <= token
        last = jnp.where(seen, scores[i * 256 :], -jnp.inf)
        scores = jnp.concatenate([scores[: i * 256], last], axis=0) if i else last
        peak = jnp.max(scores, axis=0, keepdims=True)
        probs = jnp.exp2((scores - peak) * C2)
        m_s[:, cols] = peak
        l_s[:, cols] = jnp.sum(probs, axis=0, keepdims=True)
        acc_s[:, cols] = jnp.dot(
            own_vt[:, 0 : (i + 1) * 256], probs.astype(BF16), preferred_element_type=F32
        )

    def far_here(half):
        arrived(far[half].at[pl.ds(0, 3)], 6 + half)
        far_f[...] = far[half][...].reshape(BLOCK, HD).astype(F32)
        far_k[...] = far_f[pl.ds(0, BLOCK // 2, stride=2), :].astype(BF16)
        far_vt[...] = far_f[pl.ds(1, BLOCK // 2, stride=2), :].astype(BF16).T

    def far_part(blocks, last):
        for i in blocks:
            cols = slice(i * COLS, (i + 1) * COLS)
            scores = dot_t(far_k[...], q_v[cols, :])
            before = m_s[:, cols]
            peak = jnp.maximum(before, jnp.max(scores, axis=0, keepdims=True))
            probs = jnp.exp2((scores - jnp.where(is_anchor, 1e38, peak)) * C2)
            rescale = jnp.where(is_anchor, 1.0, jnp.exp2((before - peak) * C2))
            weight_sum = l_s[:, cols] * rescale + jnp.sum(probs, axis=0, keepdims=True)
            mixed = acc_s[:, cols] * rescale + jnp.dot(
                far_vt[...], probs.astype(BF16), preferred_element_type=F32
            )
            if last:
                out_ref[cols, :] = (mixed * (1.0 / weight_sum)).T.astype(BF16)
            else:
                m_s[:, cols] = peak
                l_s[:, cols] = weight_sum
                acc_s[:, cols] = mixed


    def answer_self(queries, peak, weight_sum, mixed):
        arrived(akv.at[pl.ds(0, 4 * (N_Z - 1))], 9)
        pairs = akv[...].astype(F32)
        scores = dot_t(pairs[:, 0, :].astype(BF16), queries)
        token = lax.broadcasted_iota(jnp.int32, (QTOK, GROUP * QTOK), 1) // GROUP
        seen = lax.broadcasted_iota(jnp.int32, (QTOK, GROUP * QTOK), 0) <= token
        scores = jnp.where(seen, scores, -jnp.inf)
        both = jnp.maximum(peak, jnp.max(scores, axis=0, keepdims=True))
        rescale = jnp.exp2((peak - both) * C2)
        probs = jnp.exp2((scores - both) * C2)
        weight_sum = weight_sum * rescale + jnp.sum(probs, axis=0, keepdims=True)
        mixed = mixed * rescale + jnp.dot(
            pairs[:, 1, :].T.astype(BF16), probs.astype(BF16), preferred_element_type=F32
        )
        return both, weight_sum, mixed

    def local_peers():
        for d in range(15, 0, -1):
            to_z, to_rank = (z_lo + d // 4) % 4, (rank + d) % 4
            yield 4 * to_z + to_rank, ctx_at(to_rank // 2, 4 * z_hi + to_z, to_rank % 2)

    def answer_near():
        for to_y, to_k in near:
            to = ctx_at(to_y, z, to_k)
            send(aq_hbm.at[0], q_all.at[c], 16, ctx=to)
            send(ap_hbm.at[0], akv.at[c], 17, ctx=to)

    def answer_gather():
        loads[3].wait()
        loads[4].wait()
        arrived(q_all.at[pl.ds(0, 3)], 16)
        arrived(akv.at[pl.ds(0, 3)], 17)
        tokens = [pl.ds(2 * z, 2), pl.ds(2 * (N_Z + z), 2)]
        for d in FAR_FIRST:
            to = ctx_at(y, (z + d) % N_Z, k)
            for two in tokens:
                send(q_all.at[two], q_all.at[two], 8, ctx=to)

        @pl.when((rank == 0) & (z != 0))
        def _():
            for two in tokens:
                send(akv.at[two], akv.at[two], 9, ctx=0)

    def answer_part():
        arrived(q_all.at[pl.ds(0, 4 * (N_Z - 1))], 8)
        queries = q_all[...].astype(F32).reshape(GROUP * QTOK, HD).astype(BF16)
        scores = dot_t(own_k[...], queries)
        peak = jnp.max(scores, axis=0, keepdims=True)
        probs = jnp.exp2((scores - peak) * C2)
        weight_sum = jnp.sum(probs, axis=0, keepdims=True)
        mixed = jnp.dot(own_vt[...], probs.astype(BF16), preferred_element_type=F32)
        peak, weight_sum, mixed = lax.cond(
            c == 0,
            lambda: answer_self(queries, peak, weight_sum, mixed),
            lambda: (peak, weight_sum, mixed),
        )
        l_src[...] = peak * C2 + jnp.log2(weight_sum)
        o_src[...] = (mixed * (1.0 / weight_sum)).T.astype(BF16).reshape(16, 16, HD)
        for to, device in local_peers():
            send(o_src.at[to], o_recv.at[local], 10, ctx=device)
            send(l_src, l_recv.at[local], 11, ctx=device)
        o_recv[local] = o_src[local]
        l_recv[local] = l_src[...]

    def merged(parts, levels, first_lane):
        width = levels[0].shape[1]
        row = lax.broadcasted_iota(jnp.int32, (16, width), 0) + first_lane
        mine = lax.broadcasted_iota(jnp.int32, (16, width), 1) == row
        columns = [
            jnp.sum(jnp.where(mine, level, 0.0), axis=1, keepdims=True) for level in levels
        ]
        peak = functools.reduce(jnp.maximum, columns)
        weights = [jnp.exp2(column - peak) for column in columns]
        weight_sum = functools.reduce(jnp.add, weights)
        mixed = functools.reduce(
            jnp.add, [part.astype(F32) * weight for part, weight in zip(parts, weights)]
        )
        return mixed / weight_sum, peak + jnp.log2(weight_sum)

    def answer_local():
        arrived(o_recv.at[pl.ds(0, 15)], 10)
        arrived(l_recv.at[pl.ds(0, 15)], 11)
        mixed, level = merged(
            [o_recv[n] for n in range(16)], [l_recv[n] for n in range(16)], 16 * local
        )
        o2_src[...] = mixed.astype(BF16)
        row = lax.broadcasted_iota(jnp.int32, (16, HD), 0)
        lane = lax.broadcasted_iota(jnp.int32, (16, HD), 1)
        l2_src[...] = jnp.sum(jnp.where(row == lane, level, 0.0), axis=0, keepdims=True)
        for d in range(1, 4):
            to = ctx_at(y, 4 * ((z_hi + d) % 4) + z_lo, k)
            send(o2_src, o2_recv.at[z_hi], 12, ctx=to)
            send(l2_src, l2_recv.at[z_hi], 13, ctx=to)
        o2_recv[z_hi] = o2_src[...]
        l2_recv[z_hi] = l2_src[...]

    def answer_heads():
        arrived(o2_recv.at[pl.ds(0, 3)], 12)
        arrived(l2_recv.at[pl.ds(0, 3)], 13)
        mixed, _ = merged([o2_recv[n] for n in range(4)], [l2_recv[n] for n in range(4)], 0)
        h_src[...] = mixed.astype(BF16)
        for _, device in local_peers():
            send(h_src, h_all.at[local], 14, ctx=device)
        h_all[local] = h_src[...]

    def answer_project():
        arrived(h_all.at[pl.ds(0, 15)], 14)
        h_f[...] = h_all[...].reshape(GROUP * QTOK, HD).astype(F32)
        flat = jnp.concatenate(
            [h_f[pl.ds(h, QTOK, stride=GROUP), :] for h in range(GROUP)], axis=1
        ).astype(BF16)
        share = jnp.dot(flat, w_v[...], preferred_element_type=F32)
        p_src[...] = share.reshape(N_TP, QTOK // N_TP, HD)
        for d in range(1, N_TP):
            to = (p + d) % N_TP
            send(p_src.at[to], p_recv.at[p], 15, tp=to)
        p_recv[p] = p_src[p]

    def answer_sum():
        arrived(p_recv.at[pl.ds(0, N_TP - 1)], 15)
        ans_ref[...] = jnp.sum(p_recv[...], axis=0).astype(BF16)

    near_scatter(0)
    signal_z(here_sem.at[0], 2)
    answer_near()
    near_scatter(1)
    loads[0].wait()
    pairs_f[...] = pairs_v[...].reshape(2 * BLOCK, HD).astype(F32)
    own_k[...] = pairs_f[pl.ds(0, BLOCK, stride=2), :].astype(BF16)
    own_vt[...] = pairs_f[pl.ds(1, BLOCK, stride=2), :].astype(BF16).T
    loads[1].wait()
    pl.semaphore_wait(here_sem.at[0], 2)
    signal_z(here_sem.at[1], 4)
    own_part(0)
    own_part(1)
    own_part(2)
    pl.semaphore_wait(here_sem.at[1], 2)
    answer_gather()
    z_scatter(0)
    z_scatter(1)
    own_part(3)
    answer_part()
    z_gather(0)
    z_gather(1)
    answer_local()
    near_gather(0)
    near_gather(1)
    answer_heads()
    far_here(0)
    far_part(range(4), False)
    loads[2].wait()
    answer_project()
    far_here(1)
    far_part(range(4), True)
    answer_sum()

    for half in range(2):
        sent(cand[half].at[pl.ds(0, 3)], half)
        sent(z_cand[half].at[pl.ds(0, N_Z - 1)], 2 + half)
        sent(far[half].at[0, pl.ds(0, N_Z - 1)], 4 + half)
        sent(far[half].at[pl.ds(0, 3)], 6 + half)
    sent(q_all.at[pl.ds(0, 3)], 16)
    sent(akv.at[pl.ds(0, 3)], 17)
    sent(q_all.at[pl.ds(0, 4 * (N_Z - 1))], 8)

    @pl.when((rank == 0) & (z != 0))
    def _():
        sent(akv.at[pl.ds(0, 4)], 9)

    sent(o_recv.at[pl.ds(0, 15)], 10)
    sent(l_recv.at[pl.ds(0, 15)], 11)
    sent(o2_recv.at[pl.ds(0, 3)], 12)
    sent(l2_recv.at[pl.ds(0, 3)], 13)
    sent(h_all.at[pl.ds(0, 15)], 14)
    sent(p_recv.at[pl.ds(0, N_TP - 1)], 15)


def in_hbm(array):
    return pltpu.with_memory_space_constraint(array, pltpu.HBM)


def on_device(
    context_query, context_pairs, anchor_block, answer_query, answer_pairs, output_weight
):
    hbm = pl.BlockSpec(memory_space=pltpu.HBM)
    vmem = pl.BlockSpec(memory_space=pltpu.VMEM)
    out, answer_output = pl.pallas_call(
        kernel,
        out_shape=(
            jax.ShapeDtypeStruct((ROWS, HD), BF16),
            jax.ShapeDtypeStruct((QTOK // N_TP, HD), BF16),
        ),
        in_specs=[pl.BlockSpec(memory_space=pltpu.SMEM), hbm, hbm, hbm, hbm, hbm],
        out_specs=(vmem, vmem),
        scratch_shapes=[
            pltpu.VMEM((ROWS, HD), BF16),
            pltpu.VMEM((4, 2, N_Z, 16, HD), BF16),
            pltpu.VMEM((2 * BLOCK, HD), F32),
            pltpu.VMEM((GROUP * HD, HD), BF16),
            pltpu.VMEM((BLOCK, HD), BF16),
            pltpu.VMEM((HD, BLOCK), BF16),
            pltpu.VMEM((4, N_Z, 16, HD), BF16),
            pltpu.VMEM((4, N_Z, 16, HD), BF16),
            pltpu.VMEM((2, N_Z, 16, HD), BF16),
            pltpu.VMEM((N_Z, 16, HD), BF16),
            pltpu.VMEM((N_Z, 16, HD), BF16),
            pltpu.VMEM((4, N_Z, 16, HD), BF16),
            pltpu.VMEM((4, N_Z, 16, HD), BF16),
            pltpu.VMEM((BLOCK, HD), F32),
            pltpu.VMEM((BLOCK // 2, HD), BF16),
            pltpu.VMEM((HD, BLOCK // 2), BF16),
            pltpu.VMEM((1, ROWS), F32),
            pltpu.VMEM((1, ROWS), F32),
            pltpu.VMEM((HD, ROWS), F32),
            pltpu.VMEM((N_CTX, GROUP, HD), BF16),
            pltpu.VMEM((N_CTX, 2, HD), BF16),
            pltpu.VMEM((16, 16, HD), BF16),
            pltpu.VMEM((1, GROUP * QTOK), F32),
            pltpu.VMEM((16, 16, HD), BF16),
            pltpu.VMEM((16, 1, GROUP * QTOK), F32),
            pltpu.VMEM((16, HD), BF16),
            pltpu.VMEM((1, HD), F32),
            pltpu.VMEM((4, 16, HD), BF16),
            pltpu.VMEM((4, 1, HD), F32),
            pltpu.VMEM((16, HD), BF16),
            pltpu.VMEM((16, 16, HD), BF16),
            pltpu.VMEM((GROUP * QTOK, HD), F32),
            pltpu.VMEM((N_TP, QTOK // N_TP, HD), F32),
            pltpu.VMEM((N_TP, QTOK // N_TP, HD), F32),
            pltpu.SemaphoreType.REGULAR((2,)),
            pltpu.SemaphoreType.DMA((5,)),
            pltpu.SemaphoreType.DMA((18,)),
            pltpu.SemaphoreType.DMA((18,)),
        ],
        compiler_params=pltpu.CompilerParams(
            collective_id=0, has_side_effects=True, vmem_limit_bytes=40 * 1024 * 1024
        ),
        cost_estimate=pl.CostEstimate(
            flops=4 * ROWS * BLOCK * HD * 2, bytes_accessed=1 << 22, transcendentals=2 * ROWS * BLOCK
        ),
        name="two_phase_attention",
    )(
        anchor_block,
        in_hbm(context_query.reshape(ROWS, HD)),
        in_hbm(context_pairs.reshape(4, 2, N_Z, 16, HD)),
        in_hbm(answer_query),
        in_hbm(answer_pairs.reshape(1, 2, HD)),
        in_hbm(output_weight),
    )
    return out.reshape(BLOCK, GROUP, HD), answer_output


def solution(mesh):
    in_specs = (
        P("ctx", "tp", None),
        P("ctx", "tp", None, None),
        P(),
        P("ctx", "tp", None),
        P("ctx", "tp", None, None),
        P("tp", "ctx"),
    )
    out_specs = (P("ctx", "tp", None), P("tp", "ctx"))
    return jax.shard_map(
        on_device, mesh=mesh, in_specs=in_specs, out_specs=out_specs, check_vma=False
    )
```
